32 devices in a mesh: layer: 2 (over y), dp: 4 (over z), feat: 4 (over x, core).
Axes of the slice: x: 2, y: 2, z: 4, core: 2. Of those that a mesh axis runs over, the one named last changes fastest.
Arguments:
- train_rows: bfloat16 [2048, 4096], P(('layer', 'dp'), 'feat'), parts along dimension 0, may hold values from -6 to 6
- train_labels: int32 [2048, 1], P(('layer', 'dp')), parts along dimension 0, may hold values from 0 to 255
- held_rows: bfloat16 [4096, 4096], P(('layer', 'dp'), 'feat'), parts along dimension 0, may hold values from -6 to 6
- held_labels: int32 [4096], P(('layer', 'dp')), parts along dimension 0, may hold values from 0 to 255
- precision: bfloat16 [6, 4096, 256], P('layer', 'feat'), parts along dimension 0
Outputs:
- pooled_cov: float32 [8192, 4096], P(('layer', 'feat'), 'dp'), parts along dimension 0
- whitened: bfloat16 [4096, 4096], P(('layer', 'dp'), 'feat'), parts along dimension 0
- distance: float32 [4096], P(('layer', 'dp')), parts along dimension 0
The draws below stay inside these ranges and needn't reach their ends.
There are 2 independent parts, one for each index of `layer`. The reference program is written for one: setup_inputs(seed, part) draws one part's arguments, and reference() takes and returns one part's arrays. A program takes and returns all parts, laid end to end along the dimension named above; each array names one. Nothing has to cross between parts.
Inputs may be any that keep to these rules, and one draw needn't show every extreme that they name: `train_labels`: every class has at least one training row.
All inputs are finite; a program needn't handle non-finite values.
Results may differ from the reference program's by a relative error of at most 0.0004.
Values may be sent and summed in bfloat16 or wider, within the bound.
No kernel may reach another device: no remote copies, remote signals or barrier semaphores. Data moves between devices by JAX's collectives and lax.ppermute only.
A program may use at most 128 MiB of HBM per device.

```python
import math
import jax
import jax.numpy as jnp
from jax import lax

D = 4096
C = 256
BLK = 256
H_DEV = 512
ROWS = 1024
HELD = 2048


def draw_precision(key, part):
    first, second = jax.random.split(key, 2)
    base = jax.random.normal(first, (3, D, BLK), jnp.float32) * (0.5 / math.sqrt(3 * BLK))
    rows = jnp.arange(D) % BLK
    cols = jnp.arange(BLK)
    diagonal = (rows[:, None] == cols[None, :]).astype(jnp.float32)
    middle = (jnp.arange(3) == 1).astype(jnp.float32)[:, None, None]
    level = jax.random.uniform(second, (D, 1), jnp.float32, 1.0, 2.0)
    band = base + middle * diagonal[None] * level[None]
    return band.astype(jnp.bfloat16)


def set_ends(values, stream_key, least, high):
    index_at = [jax.random.randint(jax.random.fold_in(stream_key, axis), (), 0, length) for axis, length in enumerate(values.shape)]
    longest = values.shape.index(max(values.shape))
    neighbour = index_at[:longest] + [(index_at[longest] + 1) % values.shape[longest]] + index_at[longest + 1:]
    return values.at[tuple(index_at)].set(least).at[tuple(neighbour)].set(high)


def block_scale(key, dims, cuts, low, largest):
    level = 1.0
    for position, shards_of in cuts:
        heights = jax.random.uniform(jax.random.fold_in(jax.random.fold_in(key, 6), position), (shards_of,), jnp.float32, low / len(cuts), largest / len(cuts))
        level = level * jnp.repeat(jnp.exp(heights), dims[position] // shards_of).reshape((-1,) + (1,) * (len(dims) - 1 - position))
    return level


def different_ones(stream_key, rows, count, top, lift):
    ranking = jax.random.permutation(jax.random.fold_in(stream_key, 1), count)
    boost = ranking
    for power in range(3):
        boost = boost * boost // count
    boost = boost * lift // count
    chance = jax.random.randint(jax.random.fold_in(stream_key, 2), (rows, count), 0, 4096) + boost
    sure = jax.random.permutation(jax.random.fold_in(stream_key, 3), rows)[jnp.arange(count) % rows]
    chance = jnp.where(jnp.arange(rows)[:, None] == sure[None, :], 1 << 14, chance)
    merit = chance * count + jnp.arange(count)
    return lax.top_k(merit.astype(jnp.int32), top)[1].astype(jnp.int32)


def bell_draw(stream_key, extent, scale, bound, pieces=(), held_as=jnp.bfloat16):
    factor_of = block_scale(stream_key, extent, pieces, -0.22, 0.18) if pieces else 1.0
    result = jax.random.normal(stream_key, extent, jnp.float32) * scale * factor_of
    return jnp.minimum(jnp.maximum(result, -bound), bound).astype(held_as)


def setup_inputs(seed: int = 0, part: int = 0) -> dict:
    arg_keys = jax.random.split(jax.random.key(seed), 6)
    part_splits = jax.random.split(jax.random.fold_in(arg_keys[5], part), 6)
    return {
        "train_rows": bell_draw(part_splits[0], (ROWS, D), 1.0, 6.0, ((0, 4), (1, 4))),
        "train_labels": different_ones(part_splits[1], ROWS, C, 1, 0),
        "held_rows": bell_draw(part_splits[2], (HELD, D), 1.0, 6.0, ((0, 4), (1, 4))),
        "held_labels": set_ends(jax.random.randint(part_splits[3], (HELD,), 0, C), jax.random.fold_in(part_splits[3], 1), 0, C - 1).astype(jnp.int32),
        "precision": draw_precision(jax.random.fold_in(jax.random.fold_in(arg_keys[5], part), 71), part),
    }


def reference(train_rows, train_labels, held_rows, held_labels, precision):
    classes = jnp.arange(C, dtype=jnp.int32)
    onehot = (train_labels[:, 0:1] == classes[None, :]).astype(jnp.float32)
    counts = jnp.sum(onehot, axis=0)
    sums = jnp.dot(onehot.T, train_rows.astype(jnp.float32), precision=lax.Precision.HIGHEST)
    means = sums / counts[:, None]
    gram = jnp.dot(train_rows.T, train_rows, preferred_element_type=jnp.float32)
    pooled_cov = (gram - jnp.dot(sums.T, means, precision=lax.Precision.HIGHEST)) / (ROWS - C)
    nblocks = D // BLK
    bands = precision.astype(jnp.float32).reshape(3, nblocks, BLK, BLK)

    def score_block(item):
        rows, labels = item
        centred = rows.astype(jnp.float32) - means[labels]
        padded = jnp.pad(centred, ((0, 0), (BLK, BLK)))
        windows = padded.reshape(rows.shape[0], nblocks + 2, BLK)
        image = jnp.zeros((rows.shape[0], nblocks, BLK), jnp.float32)
        for k in range(3):
            image = image + jnp.einsum("rmj,mij->rmi", windows[:, k:k + nblocks], bands[k], precision=lax.Precision.HIGHEST)
        image = image.reshape(rows.shape[0], D)
        score = jnp.sum(centred * image, axis=1) / D
        return image.astype(jnp.bfloat16), score

    nparts = HELD // H_DEV
    whitened, distance = lax.map(score_block, (held_rows.reshape(nparts, H_DEV, D), held_labels.reshape(nparts, H_DEV)))
    return pooled_cov, whitened.reshape(HELD, D), distance.reshape(HELD)
```

```python
import jax
import jax.numpy as jnp
from jax import lax
from jax.experimental import pallas as pl
from jax.experimental.pallas import tpu as pltpu
from jax.sharding import PartitionSpec as P

C = 256
BLK = 256
F32 = jnp.float32
BF16 = jnp.bfloat16
VMEM = pl.BlockSpec(memory_space=pltpu.VMEM)
SMEM = pl.BlockSpec(memory_space=pltpu.SMEM)
ANY = pl.BlockSpec(memory_space=pl.ANY)
PARAMS = pltpu.CompilerParams(vmem_limit_bytes=48 * 1024 * 1024)


def padded(cells, sides, width):
    for axis, dim in sides:
        count = lax.axis_size(axis)
        ends = count - 1
        head = lax.slice_in_dim(cells, 0, width, axis=dim)
        tail = lax.slice_in_dim(cells, cells.shape[dim] - width, cells.shape[dim], axis=dim)
        cells = jnp.concatenate(
            [
                lax.ppermute(tail, axis, [(i, (i + 1) % count) for i in range(ends)]),
                cells,
                lax.ppermute(head, axis, [((i + 1) % count, i) for i in range(ends)]),
            ],
            axis=dim,
        )
    return cells


def contract_rows(left, right):
    return lax.dot_general(
        left, right, (((0,), (0,)), ((), ())), preferred_element_type=F32
    )


def contract_columns(left, right):
    return lax.dot_general(
        left, right, (((1,), (1,)), ((), ())), preferred_element_type=F32
    )


def body(train_rows, train_labels, held_rows, held_labels, precision):
    local = train_rows.shape[1]
    full = lax.all_gather(train_rows, "feat", axis=1, tiled=True)
    width = full.shape[1]
    classes = jnp.arange(C, dtype=jnp.int32)
    onehot_train = (train_labels == classes[None, :]).astype(BF16)
    local_sums = contract_rows(onehot_train, full)
    local_counts = jnp.sum(onehot_train.astype(F32), axis=0)
    sums, counts = lax.psum((local_sums, local_counts), "dp")
    means = sums / counts[:, None]
    feat_index = lax.axis_index("feat")
    dp_index = lax.axis_index("dp")
    dp_count = lax.axis_size("dp")
    ncols = width // dp_count
    block = lax.psum_scatter(
        contract_rows(full, train_rows), "dp", scatter_dimension=0, tiled=True
    ).T
    sums_rows = lax.dynamic_slice_in_dim(sums, feat_index * local, local, 1)
    means_cols = lax.dynamic_slice_in_dim(means, dp_index * ncols, ncols, 1)
    correction = lax.dot_general(
        sums_rows,
        means_cols,
        (((0,), (0,)), ((), ())),
        precision=lax.Precision.HIGHEST,
        preferred_element_type=F32,
    )
    denominator = float(train_rows.shape[0] * dp_count - C)
    pooled_cov = (block - correction) / denominator
    means_local = lax.dynamic_slice_in_dim(means, feat_index * local, local, 1)
    picked = means_local[held_labels]
    centred = held_rows.astype(F32) - picked
    extended = padded(centred, (("feat", 1),), BLK)
    held_count = held_rows.shape[0]
    nlocal = local // BLK
    windows = extended.reshape(held_count, nlocal + 2, BLK)
    bands = precision.astype(F32).reshape(3, nlocal, BLK, BLK)
    image = jnp.zeros((held_count, nlocal, BLK), F32)
    for k in range(3):
        image = image + jnp.einsum(
            "rmj,mij->rmi",
            windows[:, k : k + nlocal],
            bands[k],
            precision=lax.Precision.HIGHEST,
            preferred_element_type=F32,
        )
    image = image.reshape(held_count, local)
    partial_score = jnp.sum(centred * image, axis=1)
    distance = lax.psum(partial_score, "feat") / width
    return (pooled_cov, image.astype(BF16), distance)


def split3(value):
    high = value.astype(BF16)
    rest = value - high.astype(F32)
    middle = rest.astype(BF16)
    return high, middle, (rest - middle.astype(F32)).astype(BF16)


def onehot_rows(labels):
    classes = lax.broadcasted_iota(jnp.int32, (C, labels.shape[1]), 0)
    return (classes == labels).astype(F32)


def class_sums(label_refs, row_refs, columns):
    total = None
    counts = None
    for label_ref, row_ref in zip(label_refs, row_refs, strict=True):
        onehot = onehot_rows(label_ref[...])
        part = jnp.dot(onehot.astype(BF16), row_ref[:, columns], preferred_element_type=F32)
        number = jnp.sum(onehot, axis=1, keepdims=True)
        total = part if total is None else total + part
        counts = number if counts is None else counts + number
    return total, counts


def edge_kernel(parts, *refs):
    labels, rows = refs[:parts], refs[parts : 2 * parts]
    head_ref, tail_ref = refs[2 * parts :]
    width = rows[0].shape[1]
    sums, counts = class_sums(labels, rows, slice(0, BLK))
    head_ref[...] = sums / counts
    sums, counts = class_sums(labels, rows, slice(width - BLK, width))
    tail_ref[...] = sums / counts


def edge_means(labels, rows):
    shape = jax.ShapeDtypeStruct((C, BLK), F32)
    return pl.pallas_call(
        lambda *refs: edge_kernel(len(rows), *refs),
        out_shape=(shape, shape),
        in_specs=[VMEM] * (2 * len(rows)),
        out_specs=(VMEM, VMEM),
        compiler_params=PARAMS,
        name="edge_means",
    )(*labels, *rows)


def white_kernel(parts, *refs):
    labels, rows = refs[:parts], refs[parts : 2 * parts]
    (held_ref, left_ref, right_ref, left_means, right_means, held_labels, precision,
     white_ref, score_ref, bands) = refs[2 * parts :]
    width = held_ref.shape[1]
    for k in range(3):
        bands[:, k * BLK : (k + 1) * BLK] = precision[k]
    sums, counts = class_sums(labels, rows, slice(0, width))
    means = jnp.concatenate([left_means[...], sums / counts, right_means[...]], axis=1)
    onehot = onehot_rows(held_labels[...]).astype(BF16)
    picked = sum(contract_rows(onehot, piece) for piece in split3(means))
    held = jnp.concatenate([left_ref[...], held_ref[...], right_ref[...]], axis=1)
    centred = held.astype(F32) - picked
    pieces = split3(centred)
    score = jnp.zeros((held_ref.shape[0], 128), F32)
    for m in range(width // BLK):
        inside = slice(m * BLK, (m + 1) * BLK)
        window = slice(m * BLK, (m + 3) * BLK)
        band = bands[inside, :]
        image = sum(contract_columns(piece[:, window], band) for piece in reversed(pieces))
        white_ref[:, inside] = image.astype(BF16)
        product = centred[:, (m + 1) * BLK : (m + 2) * BLK] * image
        for lanes in range(0, BLK, 128):
            score = score + product[:, lanes : lanes + 128]
    score_ref[...] = jnp.sum(score.T, axis=0, keepdims=True)


def whiten(labels, rows, held, left, right, left_means, right_means, held_labels, precision):
    count, width = held.shape
    return pl.pallas_call(
        lambda *refs: white_kernel(len(rows), *refs),
        out_shape=(
            jax.ShapeDtypeStruct((count, width), BF16),
            jax.ShapeDtypeStruct((1, count), F32),
        ),
        in_specs=[VMEM] * (2 * len(rows) + 7),
        out_specs=(VMEM, VMEM),
        scratch_shapes=[pltpu.VMEM((width, 3 * BLK), BF16)],
        compiler_params=PARAMS,
        name="whiten",
    )(*labels, *rows, held, left, right, left_means, right_means, held_labels, precision)


def gram_kernel(parts, scale, *refs):
    role_ref = refs[0]
    labels, rows = refs[1 : 1 + parts], refs[1 + parts : 1 + 2 * parts]
    choices = [refs[1 + (2 + k) * parts : 1 + (3 + k) * parts] for k in range(4)]
    out_ref, left, right, sem = refs[1 + 6 * parts :]
    count = rows[0].shape[0]
    total = parts * count
    role = role_ref[0]
    for k, choice in enumerate(choices):

        @pl.when(role == k)
        def _():
            for p, ref in enumerate(choice):
                pltpu.make_async_copy(ref, right.at[pl.ds(p * count, count)], sem.at[p]).start()

    for p, ref in enumerate(rows):
        left[p * count : (p + 1) * count, :] = ref[...]
    sums, counts = class_sums(labels, rows, slice(0, rows[0].shape[1]))
    s1, s2, s3 = split3(sums)
    for p in range(parts):
        pltpu.make_async_copy(
            choices[0][p], right.at[pl.ds(p * count, count)], sem.at[p]
        ).wait()
    others = [right.at[pl.ds(p * count, count)] for p in range(parts)]
    sums, _ = class_sums(labels, others, slice(0, right.shape[1]))
    m1, m2, m3 = split3(-(sums / counts))
    for k, (s, m) in enumerate(((s1, m1), (s1, m2), (s2, m1), (s1, m3), (s2, m2), (s3, m1))):
        left[total + k * C : total + (k + 1) * C, :] = s
        right[total + k * C : total + (k + 1) * C, :] = m
    for t in range(0, out_ref.shape[0], BLK):
        out_ref[t : t + BLK, :] = contract_rows(left[:, t : t + BLK], right[...]) * scale


def pooled(role, labels, rows, choices, scale):
    count, width = rows[0].shape
    parts = len(rows)
    depth = parts * count + 6 * C
    return pl.pallas_call(
        lambda *refs: gram_kernel(parts, scale, *refs),
        out_shape=jax.ShapeDtypeStruct((width, width), F32),
        in_specs=[SMEM] + [VMEM] * (2 * parts) + [ANY] * (4 * parts),
        out_specs=VMEM,
        scratch_shapes=[
            pltpu.VMEM((depth, width), BF16),
            pltpu.VMEM((depth, width), BF16),
            pltpu.SemaphoreType.DMA((parts,)),
        ],
        compiler_params=PARAMS,
        name="pooled",
    )(role, *labels, *rows, *[ref for choice in choices for ref in choice])


def four_by_four(train_rows, train_labels, held_rows, held_labels, precision):
    count, width = train_rows.shape
    n = 4
    flip = {k: [(i, i ^ k) for i in range(n)] for k in (1, 2, 3)}
    to_right = [(i, i + 1) for i in range(n - 1)]
    to_left = [(i + 1, i) for i in range(n - 1)]
    owners = [(i, i) for i in range(n)]

    def hop(array, start, end):
        pairs = [(d * n + (d ^ start), d * n + (d ^ end)) for d, _ in owners]
        return lax.ppermute(array, ("dp", "feat"), pairs)

    rows = [train_rows]
    rows.append(lax.ppermute(train_rows, "dp", flip[2]))
    rows.append(lax.ppermute(train_rows, "dp", flip[1]))
    rows.append(lax.ppermute(rows[1], "dp", flip[1]))
    own_labels = train_labels.reshape(1, count)
    labels = [own_labels] + [lax.ppermute(own_labels, "dp", flip[k]) for k in (2, 1, 3)]
    left = lax.ppermute(held_rows[:, width - BLK :], "feat", to_right)
    right = lax.ppermute(held_rows[:, :BLK], "feat", to_left)
    across = [hop(r, 0, 2) for r in rows]
    beside = [hop(r, 0, 1) for r in rows]
    beyond = [hop(r, 2, 3) for r in across]
    head, tail = edge_means(labels, rows)
    left_means = lax.ppermute(tail, "feat", to_right)
    right_means = lax.ppermute(head, "feat", to_left)
    white, score = whiten(
        labels, rows, held_rows, left, right, left_means, right_means,
        held_labels.reshape(1, -1), precision,
    )
    role = (lax.axis_index("dp") ^ lax.axis_index("feat")).astype(jnp.int32).reshape(1)
    cov = pooled(role, labels, rows, (rows, beside, across, beyond), 1.0 / (n * count - C))
    scores = [score] + [lax.ppermute(score, "feat", flip[k]) for k in (1, 2, 3)]
    distance = ((scores[0] + scores[1]) + (scores[2] + scores[3])) / (n * width)
    return cov, white, distance.reshape(-1)


def solution(mesh):
    fits = mesh.shape["dp"] == 4 and mesh.shape["feat"] == 4
    return jax.shard_map(
        four_by_four if fits else body,
        mesh=mesh,
        in_specs=(
            P(("layer", "dp"), "feat"),
            P(("layer", "dp"), None),
            P(("layer", "dp"), "feat"),
            P(("layer", "dp")),
            P("layer", "feat", None),
        ),
        out_specs=(P(("layer", "feat"), "dp"), P(("layer", "dp"), "feat"), P(("layer", "dp"))),
        check_vma=False,
    )
```

```python
import jax
import jax.numpy as jnp
from jax import lax
from jax.experimental import pallas as pl
from jax.experimental.pallas import tpu as pltpu
from jax.sharding import PartitionSpec as P

C = 256
BLK = 256
LONG = 10**11
EXTRA = 16
F32 = jnp.float32
BF16 = jnp.bfloat16
VMEM = pl.BlockSpec(memory_space=pltpu.VMEM)
SMEM = pl.BlockSpec(memory_space=pltpu.SMEM)
ANY = pl.BlockSpec(memory_space=pl.ANY)
HBM = pl.BlockSpec(memory_space=pltpu.HBM)
SMALL = pltpu.CompilerParams(vmem_limit_bytes=8 * 1024 * 1024)
MEDIUM = pltpu.CompilerParams(vmem_limit_bytes=20 * 1024 * 1024)
LARGE = pltpu.CompilerParams(vmem_limit_bytes=24 * 1024 * 1024)


def padded(cells, sides, width):
    for axis, dim in sides:
        count = lax.axis_size(axis)
        ends = count - 1
        head = lax.slice_in_dim(cells, 0, width, axis=dim)
        tail = lax.slice_in_dim(cells, cells.shape[dim] - width, cells.shape[dim], axis=dim)
        cells = jnp.concatenate(
            [
                lax.ppermute(tail, axis, [(i, (i + 1) % count) for i in range(ends)]),
                cells,
                lax.ppermute(head, axis, [((i + 1) % count, i) for i in range(ends)]),
            ],
            axis=dim,
        )
    return cells


def contract_rows(left, right):
    return lax.dot_general(
        left, right, (((0,), (0,)), ((), ())), preferred_element_type=F32
    )


def contract_columns(left, right):
    return lax.dot_general(
        left, right, (((1,), (1,)), ((), ())), preferred_element_type=F32
    )


def body(train_rows, train_labels, held_rows, held_labels, precision):
    local = train_rows.shape[1]
    full = lax.all_gather(train_rows, "feat", axis=1, tiled=True)
    width = full.shape[1]
    classes = jnp.arange(C, dtype=jnp.int32)
    onehot_train = (train_labels == classes[None, :]).astype(BF16)
    local_sums = contract_rows(onehot_train, full)
    local_counts = jnp.sum(onehot_train.astype(F32), axis=0)
    sums, counts = lax.psum((local_sums, local_counts), "dp")
    means = sums / counts[:, None]
    feat_index = lax.axis_index("feat")
    dp_index = lax.axis_index("dp")
    dp_count = lax.axis_size("dp")
    ncols = width // dp_count
    block = lax.psum_scatter(
        contract_rows(full, train_rows), "dp", scatter_dimension=0, tiled=True
    ).T
    sums_rows = lax.dynamic_slice_in_dim(sums, feat_index * local, local, 1)
    means_cols = lax.dynamic_slice_in_dim(means, dp_index * ncols, ncols, 1)
    correction = lax.dot_general(
        sums_rows,
        means_cols,
        (((0,), (0,)), ((), ())),
        precision=lax.Precision.HIGHEST,
        preferred_element_type=F32,
    )
    denominator = float(train_rows.shape[0] * dp_count - C)
    pooled_cov = (block - correction) / denominator
    means_local = lax.dynamic_slice_in_dim(means, feat_index * local, local, 1)
    picked = means_local[held_labels]
    centred = held_rows.astype(F32) - picked
    extended = padded(centred, (("feat", 1),), BLK)
    held_count = held_rows.shape[0]
    nlocal = local // BLK
    windows = extended.reshape(held_count, nlocal + 2, BLK)
    bands = precision.astype(F32).reshape(3, nlocal, BLK, BLK)
    image = jnp.zeros((held_count, nlocal, BLK), F32)
    for k in range(3):
        image = image + jnp.einsum(
            "rmj,mij->rmi",
            windows[:, k : k + nlocal],
            bands[k],
            precision=lax.Precision.HIGHEST,
            preferred_element_type=F32,
        )
    image = image.reshape(held_count, local)
    partial_score = jnp.sum(centred * image, axis=1)
    distance = lax.psum(partial_score, "feat") / width
    return (pooled_cov, image.astype(BF16), distance)


def split3(value):
    high = value.astype(BF16)
    rest = value - high.astype(F32)
    middle = rest.astype(BF16)
    return high, middle, (rest - middle.astype(F32)).astype(BF16)


def onehot_rows(labels):
    classes = lax.broadcasted_iota(jnp.int32, (C, labels.shape[1]), 0)
    return (classes.astype(F32) == labels.astype(F32)).astype(F32)


def cost(flops):
    return pl.CostEstimate(flops=flops, bytes_accessed=0, transcendentals=0)


def class_sums(label_refs, row_refs, columns):
    total = None
    counts = None
    for label_ref, row_ref in zip(label_refs, row_refs, strict=True):
        onehot = onehot_rows(label_ref[...])
        part = jnp.dot(onehot.astype(BF16), row_ref[:, columns], preferred_element_type=F32)
        number = jnp.sum(onehot, axis=1, keepdims=True)
        total = part if total is None else total + part
        counts = number if counts is None else counts + number
    return total, counts


def fetch(sem, *pairs):
    copies = [
        pltpu.make_async_copy(source, target, sem.at[k]) for k, (source, target) in enumerate(pairs)
    ]
    for copy in copies:
        copy.start()
    return copies


def wait(copies):
    for copy in copies:
        copy.wait()


def outgoing_kernel(labels_ref, held_ref, labels_out, head_ref, tail_ref, sem):
    width = held_ref.shape[1]
    wait(
        fetch(
            sem,
            (labels_ref, labels_out),
            (held_ref.at[:, pl.ds(0, BLK)], head_ref),
            (held_ref.at[:, pl.ds(width - BLK, BLK)], tail_ref),
        )
    )


def outgoing(labels, held):
    edge = jax.ShapeDtypeStruct((held.shape[0], BLK), BF16)
    return pl.pallas_call(
        outgoing_kernel,
        out_shape=(jax.ShapeDtypeStruct(labels.shape, labels.dtype), edge, edge),
        in_specs=[HBM] * 2,
        out_specs=(VMEM,) * 3,
        scratch_shapes=[pltpu.SemaphoreType.DMA((3,))],
        compiler_params=SMALL,
        cost_estimate=cost(LONG),
        name="outgoing",
    )(labels, held)


def halves_kernel(own_ref, next_ref, rows_ref, outer_ref, inner_ref, labels, sem):
    count, width = rows_ref.shape
    copies = fetch(
        sem,
        (own_ref, labels.at[pl.ds(0, 1)]),
        (next_ref, labels.at[pl.ds(1, 1)]),
        (rows_ref.at[:, pl.ds(0, BLK)], outer_ref.at[pl.ds(0, count), pl.ds(0, BLK)]),
        (rows_ref.at[:, pl.ds(width - BLK, BLK)], outer_ref.at[pl.ds(0, count), pl.ds(BLK, BLK)]),
        (rows_ref.at[:, pl.ds(BLK, width - 2 * BLK)], inner_ref),
    )
    wait(copies[:2])
    index = lax.broadcasted_iota(jnp.int32, (EXTRA, count), 0)
    rows = jnp.where(index == 0, labels[0:1], jnp.where(index == 1, labels[1:2], 0))
    outer_ref[count : count + EXTRA, :count] = rows.astype(F32).astype(BF16)
    outer_ref[count : count + EXTRA, count:] = jnp.zeros((EXTRA, 2 * BLK - count), BF16)
    wait(copies[2:])


def halves(own_labels, next_labels, rows):
    count, width = rows.shape
    return pl.pallas_call(
        halves_kernel,
        out_shape=(
            jax.ShapeDtypeStruct((count + EXTRA, 2 * BLK), rows.dtype),
            jax.ShapeDtypeStruct((count, width - 2 * BLK), rows.dtype),
        ),
        in_specs=[HBM] * 3,
        out_specs=(VMEM, VMEM),
        scratch_shapes=[pltpu.VMEM((2, count), jnp.int32), pltpu.SemaphoreType.DMA((5,))],
        compiler_params=SMALL,
        cost_estimate=cost(1),
        name="halves",
    )(own_labels, next_labels, rows)


def early_kernel(own_label, next_label, own_ref, other_ref, sums_ref, labels, own, other, sem):
    width = own_ref.shape[1]
    copies = fetch(
        sem,
        (own_label, labels.at[pl.ds(0, 1)]),
        (next_label, labels.at[pl.ds(1, 1)]),
        (own_ref, own),
        (other_ref, other),
    )
    wait(copies)
    pairs = [labels.at[p : p + 1] for p in range(2)]
    sums, _ = class_sums(pairs, [own, other], slice(0, width))
    sums_ref[...] = sums


def early_sums(own_labels, next_labels, own, other):
    count, width = own.shape
    return pl.pallas_call(
        early_kernel,
        out_shape=jax.ShapeDtypeStruct((C, width), F32),
        in_specs=[HBM] * 4,
        out_specs=VMEM,
        scratch_shapes=[
            pltpu.VMEM((2, count), jnp.int32),
            pltpu.VMEM((count, width), BF16),
            pltpu.VMEM((count, width), BF16),
            pltpu.SemaphoreType.DMA((4,)),
        ],
        compiler_params=SMALL,
        cost_estimate=cost(LONG),
        name="early_sums",
    )(own_labels, next_labels, own, other)


def four_labels(labels, outer):
    count = labels.shape[1]
    late = outer[count : count + EXTRA, :count].astype(F32)
    return labels[0:1].astype(F32), labels[1:2].astype(F32), late[0:1], late[1:2]


def edges_kernel(own_ref, next_ref, early_ref, third_ref, outer_ref, head_ref, tail_ref,
                 labels, third, outer, sem):
    count, width = third_ref.shape
    copies = fetch(
        sem,
        (own_ref, labels.at[pl.ds(0, 1)]),
        (next_ref, labels.at[pl.ds(1, 1)]),
        (outer_ref, outer),
        (third_ref.at[:, pl.ds(0, BLK)], third.at[:, pl.ds(0, BLK)]),
        (third_ref.at[:, pl.ds(width - BLK, BLK)], third.at[:, pl.ds(BLK, BLK)]),
    )
    wait(copies[:3])
    hots = [onehot_rows(label) for label in four_labels(labels, outer)]
    counts = sum(jnp.sum(hot, axis=1, keepdims=True) for hot in hots)
    late = jnp.dot(hots[3].astype(BF16), outer[:count, :], preferred_element_type=F32)
    wait(copies[3:])
    late = late + jnp.dot(hots[2].astype(BF16), third[...], preferred_element_type=F32)
    head_ref[...] = (early_ref[:, :BLK] + late[:, :BLK]) / counts
    tail_ref[...] = (early_ref[:, width - BLK :] + late[:, BLK:]) / counts


def edge_means(own_labels, next_labels, early, third, outer):
    edge = jax.ShapeDtypeStruct((C, BLK), F32)
    count = third.shape[0]
    return pl.pallas_call(
        edges_kernel,
        out_shape=(edge, edge),
        in_specs=[HBM, HBM, VMEM, HBM, HBM],
        out_specs=(VMEM, VMEM),
        scratch_shapes=[
            pltpu.VMEM((2, count), jnp.int32),
            pltpu.VMEM((count, 2 * BLK), BF16),
            pltpu.VMEM(outer.shape, BF16),
            pltpu.SemaphoreType.DMA((5,)),
        ],
        compiler_params=SMALL,
        cost_estimate=cost(1),
        name="edge_means",
    )(own_labels, next_labels, early, third, outer)


def means_kernel(own_ref, next_ref, early_ref, third_ref, outer_ref, inner_ref,
                 means_ref, fourth_ref, labels_ref, labels, third, outer, inner, sem):
    count, width = third_ref.shape
    wait(
        fetch(
            sem,
            (own_ref, labels.at[pl.ds(0, 1)]),
            (next_ref, labels.at[pl.ds(1, 1)]),
            (third_ref, third),
            (outer_ref, outer),
            (inner_ref, inner),
        )
    )
    groups = four_labels(labels, outer)
    hots = [onehot_rows(label) for label in groups]
    counts = sum(jnp.sum(hot, axis=1, keepdims=True) for hot in hots)
    fourth = jnp.concatenate([outer[:count, :BLK], inner[...], outer[:count, BLK:]], axis=1)
    fourth_ref[...] = fourth
    sums = early_ref[...] + jnp.dot(hots[2].astype(BF16), third[...], preferred_element_type=F32)
    sums = sums + jnp.dot(hots[3].astype(BF16), fourth, preferred_element_type=F32)
    means_ref[...] = sums / counts
    for p, label in enumerate(groups):
        labels_ref[p : p + 1, :] = label


def class_means(own_labels, next_labels, early, third, outer, inner):
    whole = jax.ShapeDtypeStruct(early.shape, F32)
    count = third.shape[0]
    return pl.pallas_call(
        means_kernel,
        out_shape=(
            whole,
            jax.ShapeDtypeStruct(third.shape, third.dtype),
            jax.ShapeDtypeStruct((4, count), F32),
        ),
        in_specs=[HBM, HBM, VMEM, HBM, HBM, HBM],
        out_specs=(VMEM,) * 3,
        scratch_shapes=[
            pltpu.VMEM((2, count), jnp.int32),
            pltpu.VMEM(third.shape, BF16),
            pltpu.VMEM(outer.shape, BF16),
            pltpu.VMEM(inner.shape, BF16),
            pltpu.SemaphoreType.DMA((5,)),
        ],
        compiler_params=MEDIUM,
        cost_estimate=cost(LONG),
        name="class_means",
    )(own_labels, next_labels, early, third, outer, inner)


def stack_kernel(groups, role_ref, *refs):
    *sources, out_ref, sem = refs
    groups = (sources[: groups[0]], sources[groups[0] :])

    def pairs(group):
        start = 0
        for ref in group:
            yield ref, out_ref.at[pl.ds(start, ref.shape[0])]
            start += ref.shape[0]

    for owner, group in zip((True, False), groups, strict=True):

        @pl.when((role_ref[0] == 0) == owner)
        def _():
            wait(fetch(sem, *pairs(group)))


def stack(role, own, other):
    rows = sum(array.shape[0] for array in own)
    groups = (len(own), len(other))
    return pl.pallas_call(
        lambda *refs: stack_kernel(groups, *refs),
        out_shape=jax.ShapeDtypeStruct((rows, own[0].shape[1]), own[0].dtype),
        in_specs=[SMEM] + [ANY] * sum(groups),
        out_specs=ANY,
        scratch_shapes=[pltpu.SemaphoreType.DMA((max(groups),))],
        compiler_params=SMALL,
        cost_estimate=cost(1),
        name="stack",
    )(role, *own, *other)


def white_kernel(held_ref, left_ref, right_ref, means_ref, left_means, right_means, held_labels,
                 precision, white_ref, score_ref, bands):
    width = held_ref.shape[1]
    for k in range(3):
        bands[:, k * BLK : (k + 1) * BLK] = precision[k]
    means = jnp.concatenate([left_means[...], means_ref[...], right_means[...]], axis=1)
    onehot = onehot_rows(held_labels[...]).astype(BF16)
    picked = sum(contract_rows(onehot, piece) for piece in split3(means))
    held = jnp.concatenate([left_ref[...], held_ref[...], right_ref[...]], axis=1)
    centred = held.astype(F32) - picked
    pieces = split3(centred)
    score = jnp.zeros((held_ref.shape[0], 128), F32)
    for m in range(width // BLK):
        inside = slice(m * BLK, (m + 1) * BLK)
        window = slice(m * BLK, (m + 3) * BLK)
        band = bands[inside, :]
        image = sum(contract_columns(piece[:, window], band) for piece in reversed(pieces))
        white_ref[:, inside] = image.astype(BF16)
        product = centred[:, (m + 1) * BLK : (m + 2) * BLK] * image
        for lanes in range(0, BLK, 128):
            score = score + product[:, lanes : lanes + 128]
    score_ref[...] = jnp.sum(score.T, axis=0, keepdims=True)


def whiten(held, left, right, means, left_means, right_means, held_labels, precision):
    count, width = held.shape
    return pl.pallas_call(
        white_kernel,
        out_shape=(
            jax.ShapeDtypeStruct((count, width), BF16),
            jax.ShapeDtypeStruct((1, count), F32),
        ),
        in_specs=[VMEM] * 8,
        out_specs=(VMEM, VMEM),
        scratch_shapes=[pltpu.VMEM((width, 3 * BLK), BF16)],
        compiler_params=MEDIUM,
        cost_estimate=cost(LONG),
        name="whiten",
    )(held, left, right, means, left_means, right_means, held_labels, precision)


def choose(role_ref, sem, near, far, target):
    here = (role_ref[0] % 2) == 0

    @pl.when(here)
    def _():
        fetch(sem, (near, target))

    @pl.when(jnp.logical_not(here))
    def _():
        fetch(sem, (far, target))

    return pltpu.make_async_copy(near, target, sem.at[0])


def centre_kernel(labels_ref, means_ref, *refs):
    *rows, most_ref, last_ref = refs
    count = rows[0].shape[0]
    most = most_ref.shape[0] // 2
    pieces = split3(means_ref[...])
    for p, ref in enumerate(rows):
        onehot = onehot_rows(labels_ref[p : p + 1]).astype(BF16)
        centred = ref[...].astype(F32) - sum(contract_rows(onehot, piece) for piece in pieces)
        high = centred.astype(BF16)
        low = (centred - high.astype(F32)).astype(BF16)
        into, first, second = (most_ref, p * count, most + p * count)
        if p == len(rows) - 1:
            into, first, second = (last_ref, 0, count)
        into[first : first + count, :] = high
        into[second : second + count, :] = low


def centre(labels, means, rows):
    count, width = rows[0].shape
    return pl.pallas_call(
        centre_kernel,
        out_shape=(
            jax.ShapeDtypeStruct((2 * (len(rows) - 1) * count, width), BF16),
            jax.ShapeDtypeStruct((2 * count, width), BF16),
        ),
        in_specs=[VMEM] * (2 + len(rows)),
        out_specs=(VMEM, VMEM),
        compiler_params=MEDIUM,
        cost_estimate=cost(1),
        name="centre",
    )(labels, means, *rows)


def most_kernel(role_ref, left, near, far, total_ref, right, sem):
    most, width = near.shape
    choose(role_ref, sem, near, far, right).wait()
    for t in range(0, width, BLK):
        high = contract_rows(left[:most, t : t + BLK], right[...])
        total_ref[t : t + BLK, :] = high + contract_rows(left[most:, t : t + BLK], right[...])


def gram_most(role, centred, near, far):
    width = near.shape[1]
    return pl.pallas_call(
        most_kernel,
        out_shape=jax.ShapeDtypeStruct((width, width), F32),
        in_specs=[SMEM, VMEM, ANY, ANY],
        out_specs=VMEM,
        scratch_shapes=[pltpu.VMEM(near.shape, BF16), pltpu.SemaphoreType.DMA((1,))],
        compiler_params=MEDIUM,
        cost_estimate=cost(LONG),
        name="gram_most",
    )(role, centred, near, far)


def last_kernel(scale, features, role_ref, total_ref, last_ref, near, far, own, *refs):
    *others, out_ref, distance_ref, right, tiles, sem, out_sem = refs
    count, width = near.shape
    arrival = choose(role_ref, sem, near, far, right)
    beside, across, beyond = [ref[...] for ref in others]
    distance_ref[...] = ((own[...] + beside) + (across + beyond)) / features
    arrival.wait()
    stores = []
    for k, t in enumerate(range(0, width, BLK)):
        part = contract_rows(last_ref[:count, t : t + BLK], right[...])
        part = part + contract_rows(last_ref[count:, t : t + BLK], right[...])
        tiles[t : t + BLK, :] = (total_ref[t : t + BLK, :] + part) * scale
        stores.append(
            pltpu.make_async_copy(
                tiles.at[pl.ds(t, BLK)], out_ref.at[pl.ds(t, BLK)], out_sem.at[k]
            )
        )
        stores[-1].start()
    wait(stores)


def gram_last(role, total, last, near, far, scores, scale, features):
    count, width = near.shape
    return pl.pallas_call(
        lambda *refs: last_kernel(scale, features, *refs),
        out_shape=(
            jax.ShapeDtypeStruct((width, width), F32),
            jax.ShapeDtypeStruct(scores[0].shape, F32),
        ),
        in_specs=[SMEM, VMEM, VMEM, ANY, ANY] + [VMEM] * len(scores),
        out_specs=(HBM, VMEM),
        scratch_shapes=[
            pltpu.VMEM((count, width), BF16),
            pltpu.VMEM((width, width), F32),
            pltpu.SemaphoreType.DMA((1,)),
            pltpu.SemaphoreType.DMA((width // BLK,)),
        ],
        compiler_params=MEDIUM,
        cost_estimate=cost(LONG),
        name="gram_last",
    )(role, total, last, near, far, *scores)


def four_by_four(train_rows, train_labels, held_rows, held_labels, precision):
    count, width = train_rows.shape
    n = 4
    tie = lax.optimization_barrier
    flip = {k: [(i, i ^ k) for i in range(n)] for k in (1, 2, 3)}
    to_right = [(i, i + 1) for i in range(n - 1)]
    to_left = [(i + 1, i) for i in range(n - 1)]
    role = (lax.axis_index("dp") ^ lax.axis_index("feat")).astype(jnp.int32)

    def hop(array, *moves):
        pairs = [(d * n + (d ^ s), d * n + (d ^ e)) for d in range(n) for s, e in moves]
        return lax.ppermute(array, ("dp", "feat"), pairs)

    across_own = hop(train_rows, (0, 2))
    third = lax.ppermute(train_rows, "dp", flip[1])
    second = lax.ppermute(train_rows, "dp", flip[2])
    own_labels, head, tail = outgoing(train_labels.reshape(1, count), held_rows)
    next_labels = lax.ppermute(own_labels, "dp", flip[2])
    left = lax.ppermute(tail, "feat", to_right)
    third, second, across_own, left, next_labels = tie(
        (third, second, across_own, left, next_labels)
    )
    second_outer, second_inner = halves(own_labels, next_labels, second)
    outer = lax.ppermute(second_outer, "dp", flip[1])
    inner = lax.ppermute(second_inner, "dp", flip[1])
    early = early_sums(own_labels, next_labels, train_rows, second)
    early, head, *sent = tie((early, head, second, third))
    role = role.reshape(1)
    own_most = stack(role, sent, sent)
    across_most = hop(own_most, (0, 2))
    right = lax.ppermute(head, "feat", to_left)
    head, tail = edge_means(own_labels, next_labels, early, third, outer)
    left_means = lax.ppermute(tail, "feat", to_right)
    right_means = lax.ppermute(head, "feat", to_left)
    inner, across_most, right, head, tail = tie((inner, across_most, right, head, tail))
    means, fourth, labels = class_means(own_labels, next_labels, early, third, outer, inner)
    across_last = hop(fourth, (0, 2))
    rows = [train_rows, second, third, fourth]
    near_most = stack(role, rows[:3], [across_own, across_most])
    far_most = hop(near_most, (0, 1), (2, 3))
    most, last = centre(labels, means, rows)
    most, last, means = tie((most, last, means))
    white, score = whiten(
        held_rows, left, right, means, left_means, right_means, held_labels.reshape(1, -1), precision
    )
    score, across_last, most = tie((score, across_last, most))
    total = gram_most(role, most, near_most, far_most)
    near_last = stack(role, [fourth], [across_last])
    far_last = hop(near_last, (0, 1), (2, 3))
    scores = [score] + [lax.ppermute(score, "feat", flip[k]) for k in (1, 2, 3)]
    cov, distance = gram_last(
        role, total, last, near_last, far_last, scores, 1.0 / (n * count - C), float(n * width)
    )
    return cov, white, distance.reshape(-1)


def solution(mesh):
    fits = mesh.shape["dp"] == 4 and mesh.shape["feat"] == 4
    return jax.shard_map(
        four_by_four if fits else body,
        mesh=mesh,
        in_specs=(
            P(("layer", "dp"), "feat"),
            P(("layer", "dp"), None),
            P(("layer", "dp"), "feat"),
            P(("layer", "dp")),
            P("layer", "feat", None),
        ),
        out_specs=(P(("layer", "feat"), "dp"), P(("layer", "dp"), "feat"), P(("layer", "dp"))),
        check_vma=False,
    )
```

```python
import jax
import jax.numpy as jnp
from jax import lax
from jax.experimental import pallas as pl
from jax.experimental.pallas import tpu as pltpu
from jax.sharding import PartitionSpec as P

C = 256
BLK = 256
LONG = 10**11
EXTRA = 16
TILE = 128
F32 = jnp.float32
BF16 = jnp.bfloat16
VMEM = pl.BlockSpec(memory_space=pltpu.VMEM)
SMEM = pl.BlockSpec(memory_space=pltpu.SMEM)
ANY = pl.BlockSpec(memory_space=pl.ANY)
HBM = pl.BlockSpec(memory_space=pltpu.HBM)
SMALL = pltpu.CompilerParams(vmem_limit_bytes=8 * 1024 * 1024)
MEDIUM = pltpu.CompilerParams(vmem_limit_bytes=20 * 1024 * 1024)
LARGE = pltpu.CompilerParams(vmem_limit_bytes=24 * 1024 * 1024)


def padded(cells, sides, width):
    for axis, dim in sides:
        count = lax.axis_size(axis)
        ends = count - 1
        head = lax.slice_in_dim(cells, 0, width, axis=dim)
        tail = lax.slice_in_dim(cells, cells.shape[dim] - width, cells.shape[dim], axis=dim)
        cells = jnp.concatenate(
            [
                lax.ppermute(tail, axis, [(i, (i + 1) % count) for i in range(ends)]),
                cells,
                lax.ppermute(head, axis, [((i + 1) % count, i) for i in range(ends)]),
            ],
            axis=dim,
        )
    return cells


def contract_rows(left, right):
    return lax.dot_general(
        left, right, (((0,), (0,)), ((), ())), preferred_element_type=F32
    )


def contract_columns(left, right):
    return lax.dot_general(
        left, right, (((1,), (1,)), ((), ())), preferred_element_type=F32
    )


def body(train_rows, train_labels, held_rows, held_labels, precision):
    local = train_rows.shape[1]
    full = lax.all_gather(train_rows, "feat", axis=1, tiled=True)
    width = full.shape[1]
    classes = jnp.arange(C, dtype=jnp.int32)
    onehot_train = (train_labels == classes[None, :]).astype(BF16)
    local_sums = contract_rows(onehot_train, full)
    local_counts = jnp.sum(onehot_train.astype(F32), axis=0)
    sums, counts = lax.psum((local_sums, local_counts), "dp")
    means = sums / counts[:, None]
    feat_index = lax.axis_index("feat")
    dp_index = lax.axis_index("dp")
    dp_count = lax.axis_size("dp")
    ncols = width // dp_count
    block = lax.psum_scatter(
        contract_rows(full, train_rows), "dp", scatter_dimension=0, tiled=True
    ).T
    sums_rows = lax.dynamic_slice_in_dim(sums, feat_index * local, local, 1)
    means_cols = lax.dynamic_slice_in_dim(means, dp_index * ncols, ncols, 1)
    correction = lax.dot_general(
        sums_rows,
        means_cols,
        (((0,), (0,)), ((), ())),
        precision=lax.Precision.HIGHEST,
        preferred_element_type=F32,
    )
    denominator = float(train_rows.shape[0] * dp_count - C)
    pooled_cov = (block - correction) / denominator
    means_local = lax.dynamic_slice_in_dim(means, feat_index * local, local, 1)
    picked = means_local[held_labels]
    centred = held_rows.astype(F32) - picked
    extended = padded(centred, (("feat", 1),), BLK)
    held_count = held_rows.shape[0]
    nlocal = local // BLK
    windows = extended.reshape(held_count, nlocal + 2, BLK)
    bands = precision.astype(F32).reshape(3, nlocal, BLK, BLK)
    image = jnp.zeros((held_count, nlocal, BLK), F32)
    for k in range(3):
        image = image + jnp.einsum(
            "rmj,mij->rmi",
            windows[:, k : k + nlocal],
            bands[k],
            precision=lax.Precision.HIGHEST,
            preferred_element_type=F32,
        )
    image = image.reshape(held_count, local)
    partial_score = jnp.sum(centred * image, axis=1)
    distance = lax.psum(partial_score, "feat") / width
    return (pooled_cov, image.astype(BF16), distance)


def split3(value):
    high = value.astype(BF16)
    rest = value - high.astype(F32)
    middle = rest.astype(BF16)
    return high, middle, (rest - middle.astype(F32)).astype(BF16)


def onehot_rows(labels):
    classes = lax.broadcasted_iota(jnp.int32, (C, labels.shape[1]), 0)
    return (classes.astype(F32) == labels.astype(F32)).astype(F32)


def cost(flops):
    return pl.CostEstimate(flops=flops, bytes_accessed=0, transcendentals=0)


def class_sums(label_refs, row_refs, columns):
    total = None
    counts = None
    for label_ref, row_ref in zip(label_refs, row_refs, strict=True):
        onehot = onehot_rows(label_ref[...])
        part = jnp.dot(onehot.astype(BF16), row_ref[:, columns], preferred_element_type=F32)
        number = jnp.sum(onehot, axis=1, keepdims=True)
        total = part if total is None else total + part
        counts = number if counts is None else counts + number
    return total, counts


def fetch(sem, *pairs):
    copies = [
        pltpu.make_async_copy(source, target, sem.at[k]) for k, (source, target) in enumerate(pairs)
    ]
    for copy in copies:
        copy.start()
    return copies


def wait(copies):
    for copy in copies:
        copy.wait()


def outgoing_kernel(labels_ref, held_ref, labels_out, head_ref, tail_ref, sem):
    width = held_ref.shape[1]
    wait(
        fetch(
            sem,
            (labels_ref, labels_out),
            (held_ref.at[:, pl.ds(0, BLK)], head_ref),
            (held_ref.at[:, pl.ds(width - BLK, BLK)], tail_ref),
        )
    )


def outgoing(labels, held):
    edge = jax.ShapeDtypeStruct((held.shape[0], BLK), BF16)
    return pl.pallas_call(
        outgoing_kernel,
        out_shape=(jax.ShapeDtypeStruct(labels.shape, labels.dtype), edge, edge),
        in_specs=[HBM] * 2,
        out_specs=(VMEM,) * 3,
        scratch_shapes=[pltpu.SemaphoreType.DMA((3,))],
        compiler_params=SMALL,
        cost_estimate=cost(LONG),
        name="outgoing",
    )(labels, held)


def halves_kernel(own_ref, next_ref, rows_ref, outer_ref, inner_ref, labels, sem):
    count, width = rows_ref.shape
    copies = fetch(
        sem,
        (own_ref, labels.at[pl.ds(0, 1)]),
        (next_ref, labels.at[pl.ds(1, 1)]),
        (rows_ref.at[:, pl.ds(0, BLK)], outer_ref.at[pl.ds(0, count), pl.ds(0, BLK)]),
        (rows_ref.at[:, pl.ds(width - BLK, BLK)], outer_ref.at[pl.ds(0, count), pl.ds(BLK, BLK)]),
        (rows_ref.at[:, pl.ds(BLK, width - 2 * BLK)], inner_ref),
    )
    wait(copies[:2])
    index = lax.broadcasted_iota(jnp.int32, (EXTRA, count), 0)
    rows = jnp.where(index == 0, labels[0:1], jnp.where(index == 1, labels[1:2], 0))
    outer_ref[count : count + EXTRA, :count] = rows.astype(F32).astype(BF16)
    outer_ref[count : count + EXTRA, count:] = jnp.zeros((EXTRA, 2 * BLK - count), BF16)
    wait(copies[2:])


def halves(own_labels, next_labels, rows):
    count, width = rows.shape
    return pl.pallas_call(
        halves_kernel,
        out_shape=(
            jax.ShapeDtypeStruct((count + EXTRA, 2 * BLK), rows.dtype),
            jax.ShapeDtypeStruct((count, width - 2 * BLK), rows.dtype),
        ),
        in_specs=[HBM] * 3,
        out_specs=(VMEM, VMEM),
        scratch_shapes=[pltpu.VMEM((2, count), jnp.int32), pltpu.SemaphoreType.DMA((5,))],
        compiler_params=SMALL,
        cost_estimate=cost(1),
        name="halves",
    )(own_labels, next_labels, rows)


def early_kernel(own_label, next_label, own_ref, other_ref, sums_ref, labels, own, other, sem):
    width = own_ref.shape[1]
    copies = fetch(
        sem,
        (own_label, labels.at[pl.ds(0, 1)]),
        (next_label, labels.at[pl.ds(1, 1)]),
        (own_ref, own),
        (other_ref, other),
    )
    wait(copies)
    pairs = [labels.at[p : p + 1] for p in range(2)]
    sums, _ = class_sums(pairs, [own, other], slice(0, width))
    sums_ref[...] = sums


def early_sums(own_labels, next_labels, own, other):
    count, width = own.shape
    return pl.pallas_call(
        early_kernel,
        out_shape=jax.ShapeDtypeStruct((C, width), F32),
        in_specs=[HBM] * 4,
        out_specs=VMEM,
        scratch_shapes=[
            pltpu.VMEM((2, count), jnp.int32),
            pltpu.VMEM((count, width), BF16),
            pltpu.VMEM((count, width), BF16),
            pltpu.SemaphoreType.DMA((4,)),
        ],
        compiler_params=SMALL,
        cost_estimate=cost(LONG),
        name="early_sums",
    )(own_labels, next_labels, own, other)


def four_labels(labels, outer):
    count = labels.shape[1]
    late = outer[count : count + EXTRA, :count].astype(F32)
    return labels[0:1].astype(F32), labels[1:2].astype(F32), late[0:1], late[1:2]


def edges_kernel(own_ref, next_ref, early_ref, third_ref, outer_ref, head_ref, tail_ref,
                 labels, third, outer, sem):
    count, width = third_ref.shape
    copies = fetch(
        sem,
        (own_ref, labels.at[pl.ds(0, 1)]),
        (next_ref, labels.at[pl.ds(1, 1)]),
        (outer_ref, outer),
        (third_ref.at[:, pl.ds(0, BLK)], third.at[:, pl.ds(0, BLK)]),
        (third_ref.at[:, pl.ds(width - BLK, BLK)], third.at[:, pl.ds(BLK, BLK)]),
    )
    wait(copies[:3])
    hots = [onehot_rows(label) for label in four_labels(labels, outer)]
    counts = sum(jnp.sum(hot, axis=1, keepdims=True) for hot in hots)
    late = jnp.dot(hots[3].astype(BF16), outer[:count, :], preferred_element_type=F32)
    wait(copies[3:])
    late = late + jnp.dot(hots[2].astype(BF16), third[...], preferred_element_type=F32)
    head_ref[...] = (early_ref[:, :BLK] + late[:, :BLK]) / counts
    tail_ref[...] = (early_ref[:, width - BLK :] + late[:, BLK:]) / counts


def edge_means(own_labels, next_labels, early, third, outer):
    edge = jax.ShapeDtypeStruct((C, BLK), F32)
    count = third.shape[0]
    return pl.pallas_call(
        edges_kernel,
        out_shape=(edge, edge),
        in_specs=[HBM, HBM, VMEM, HBM, HBM],
        out_specs=(VMEM, VMEM),
        scratch_shapes=[
            pltpu.VMEM((2, count), jnp.int32),
            pltpu.VMEM((count, 2 * BLK), BF16),
            pltpu.VMEM(outer.shape, BF16),
            pltpu.SemaphoreType.DMA((5,)),
        ],
        compiler_params=SMALL,
        cost_estimate=cost(1),
        name="edge_means",
    )(own_labels, next_labels, early, third, outer)


def means_kernel(own_ref, next_ref, early_ref, third_ref, outer_ref, inner_ref,
                 means_ref, fourth_ref, labels_ref, labels, third, outer, inner, sem):
    count, width = third_ref.shape
    wait(
        fetch(
            sem,
            (own_ref, labels.at[pl.ds(0, 1)]),
            (next_ref, labels.at[pl.ds(1, 1)]),
            (third_ref, third),
            (outer_ref, outer),
            (inner_ref, inner),
        )
    )
    groups = four_labels(labels, outer)
    hots = [onehot_rows(label) for label in groups]
    counts = sum(jnp.sum(hot, axis=1, keepdims=True) for hot in hots)
    fourth = jnp.concatenate([outer[:count, :BLK], inner[...], outer[:count, BLK:]], axis=1)
    fourth_ref[...] = fourth
    sums = early_ref[...] + jnp.dot(hots[2].astype(BF16), third[...], preferred_element_type=F32)
    sums = sums + jnp.dot(hots[3].astype(BF16), fourth, preferred_element_type=F32)
    means_ref[...] = sums / counts
    for p, label in enumerate(groups):
        labels_ref[p : p + 1, :] = label


def class_means(own_labels, next_labels, early, third, outer, inner):
    whole = jax.ShapeDtypeStruct(early.shape, F32)
    count = third.shape[0]
    return pl.pallas_call(
        means_kernel,
        out_shape=(
            whole,
            jax.ShapeDtypeStruct(third.shape, third.dtype),
            jax.ShapeDtypeStruct((4, count), F32),
        ),
        in_specs=[HBM, HBM, VMEM, HBM, HBM, HBM],
        out_specs=(VMEM,) * 3,
        scratch_shapes=[
            pltpu.VMEM((2, count), jnp.int32),
            pltpu.VMEM(third.shape, BF16),
            pltpu.VMEM(outer.shape, BF16),
            pltpu.VMEM(inner.shape, BF16),
            pltpu.SemaphoreType.DMA((5,)),
        ],
        compiler_params=MEDIUM,
        cost_estimate=cost(LONG),
        name="class_means",
    )(own_labels, next_labels, early, third, outer, inner)


def stack_kernel(groups, role_ref, *refs):
    *sources, out_ref, sem = refs
    groups = (sources[: groups[0]], sources[groups[0] :])

    def pairs(group):
        start = 0
        for ref in group:
            yield ref, out_ref.at[pl.ds(start, ref.shape[0])]
            start += ref.shape[0]

    for owner, group in zip((True, False), groups, strict=True):

        @pl.when((role_ref[0] == 0) == owner)
        def _():
            wait(fetch(sem, *pairs(group)))


def stack(role, own, other):
    rows = sum(array.shape[0] for array in own)
    groups = (len(own), len(other))
    return pl.pallas_call(
        lambda *refs: stack_kernel(groups, *refs),
        out_shape=jax.ShapeDtypeStruct((rows, own[0].shape[1]), own[0].dtype),
        in_specs=[SMEM] + [ANY] * sum(groups),
        out_specs=ANY,
        scratch_shapes=[pltpu.SemaphoreType.DMA((max(groups),))],
        compiler_params=SMALL,
        cost_estimate=cost(1),
        name="stack",
    )(role, *own, *other)


def white_kernel(held_ref, left_ref, right_ref, means_ref, left_means, right_means, held_labels,
                 precision, white_ref, score_ref, bands):
    width = held_ref.shape[1]
    for k in range(3):
        bands[:, k * BLK : (k + 1) * BLK] = precision[k]
    means = jnp.concatenate([left_means[...], means_ref[...], right_means[...]], axis=1)
    onehot = onehot_rows(held_labels[...]).astype(BF16)
    picked = sum(contract_rows(onehot, piece) for piece in split3(means))
    held = jnp.concatenate([left_ref[...], held_ref[...], right_ref[...]], axis=1)
    centred = held.astype(F32) - picked
    pieces = split3(centred)[:2]
    score = jnp.zeros((held_ref.shape[0], 128), F32)
    for m in range(width // BLK):
        inside = slice(m * BLK, (m + 1) * BLK)
        window = slice(m * BLK, (m + 3) * BLK)
        band = bands[inside, :]
        image = sum(contract_columns(piece[:, window], band) for piece in reversed(pieces))
        white_ref[:, inside] = image.astype(BF16)
        product = centred[:, (m + 1) * BLK : (m + 2) * BLK] * image
        for lanes in range(0, BLK, 128):
            score = score + product[:, lanes : lanes + 128]
    score_ref[...] = jnp.sum(score.T, axis=0, keepdims=True)


def whiten(held, left, right, means, left_means, right_means, held_labels, precision):
    count, width = held.shape
    return pl.pallas_call(
        white_kernel,
        out_shape=(
            jax.ShapeDtypeStruct((count, width), BF16),
            jax.ShapeDtypeStruct((1, count), F32),
        ),
        in_specs=[VMEM] * 8,
        out_specs=(VMEM, VMEM),
        scratch_shapes=[pltpu.VMEM((width, 3 * BLK), BF16)],
        compiler_params=MEDIUM,
        cost_estimate=cost(LONG),
        name="whiten",
    )(held, left, right, means, left_means, right_means, held_labels, precision)


def choose(role_ref, sem, near, far, target):
    here = (role_ref[0] % 2) == 0

    @pl.when(here)
    def _():
        fetch(sem, (near, target))

    @pl.when(jnp.logical_not(here))
    def _():
        fetch(sem, (far, target))

    return pltpu.make_async_copy(near, target, sem.at[0])


def centre_kernel(labels_ref, means_ref, *refs):
    *rows, most_ref, last_ref = refs
    count = rows[0].shape[0]
    most = most_ref.shape[0] // 2
    pieces = split3(means_ref[...])
    for p, ref in enumerate(rows):
        onehot = onehot_rows(labels_ref[p : p + 1]).astype(BF16)
        centred = ref[...].astype(F32) - sum(contract_rows(onehot, piece) for piece in pieces)
        high = centred.astype(BF16)
        low = (centred - high.astype(F32)).astype(BF16)
        into, first, second = (most_ref, p * count, most + p * count)
        if p == len(rows) - 1:
            into, first, second = (last_ref, 0, count)
        into[first : first + count, :] = high
        into[second : second + count, :] = low


def centre(labels, means, rows):
    count, width = rows[0].shape
    return pl.pallas_call(
        centre_kernel,
        out_shape=(
            jax.ShapeDtypeStruct((2 * (len(rows) - 1) * count, width), BF16),
            jax.ShapeDtypeStruct((2 * count, width), BF16),
        ),
        in_specs=[VMEM] * (2 + len(rows)),
        out_specs=(VMEM, VMEM),
        compiler_params=MEDIUM,
        cost_estimate=cost(1),
        name="centre",
    )(labels, means, *rows)


def most_kernel(role_ref, left, near, far, total_ref, right, sem):
    most, width = near.shape
    choose(role_ref, sem, near, far, right).wait()
    for t in range(0, width, BLK):
        high = contract_rows(left[:most, t : t + BLK], right[...])
        total_ref[t : t + BLK, :] = high + contract_rows(left[most:, t : t + BLK], right[...])


def gram_most(role, centred, near, far):
    width = near.shape[1]
    return pl.pallas_call(
        most_kernel,
        out_shape=jax.ShapeDtypeStruct((width, width), F32),
        in_specs=[SMEM, VMEM, ANY, ANY],
        out_specs=VMEM,
        scratch_shapes=[pltpu.VMEM(near.shape, BF16), pltpu.SemaphoreType.DMA((1,))],
        compiler_params=MEDIUM,
        cost_estimate=cost(LONG),
        name="gram_most",
    )(role, centred, near, far)


def last_kernel(scale, features, role_ref, total_ref, last_ref, near, far, own, *refs):
    *others, out_ref, distance_ref, right, tiles, sem, out_sem = refs
    count, width = near.shape
    arrival = choose(role_ref, sem, near, far, right)
    beside, across, beyond = [ref[...] for ref in others]
    distance_ref[...] = ((own[...] + beside) + (across + beyond)) / features
    arrival.wait()
    stores = []
    for k, t in enumerate(range(0, width, TILE)):
        part = contract_rows(last_ref[:count, t : t + TILE], right[...])
        part = part + contract_rows(last_ref[count:, t : t + TILE], right[...])
        tiles[t : t + TILE, :] = (total_ref[t : t + TILE, :] + part) * scale
        stores.append(
            pltpu.make_async_copy(
                tiles.at[pl.ds(t, TILE)], out_ref.at[pl.ds(t, TILE)], out_sem.at[k]
            )
        )
        stores[-1].start()
    wait(stores)


def gram_last(role, total, last, near, far, scores, scale, features):
    count, width = near.shape
    return pl.pallas_call(
        lambda *refs: last_kernel(scale, features, *refs),
        out_shape=(
            jax.ShapeDtypeStruct((width, width), F32),
            jax.ShapeDtypeStruct(scores[0].shape, F32),
        ),
        in_specs=[SMEM, VMEM, VMEM, ANY, ANY] + [VMEM] * len(scores),
        out_specs=(HBM, VMEM),
        scratch_shapes=[
            pltpu.VMEM((count, width), BF16),
            pltpu.VMEM((width, width), F32),
            pltpu.SemaphoreType.DMA((1,)),
            pltpu.SemaphoreType.DMA((width // TILE,)),
        ],
        compiler_params=MEDIUM,
        cost_estimate=cost(LONG),
        name="gram_last",
    )(role, total, last, near, far, *scores)


def four_by_four(train_rows, train_labels, held_rows, held_labels, precision):
    count, width = train_rows.shape
    n = 4
    tie = lax.optimization_barrier
    flip = {k: [(i, i ^ k) for i in range(n)] for k in (1, 2, 3)}
    to_right = [(i, i + 1) for i in range(n - 1)]
    to_left = [(i + 1, i) for i in range(n - 1)]
    role = (lax.axis_index("dp") ^ lax.axis_index("feat")).astype(jnp.int32)

    def hop(array, *moves):
        pairs = [(d * n + (d ^ s), d * n + (d ^ e)) for d in range(n) for s, e in moves]
        return lax.ppermute(array, ("dp", "feat"), pairs)

    across_own = hop(train_rows, (0, 2))
    third = lax.ppermute(train_rows, "dp", flip[1])
    second = lax.ppermute(train_rows, "dp", flip[2])
    own_labels, head, tail = outgoing(train_labels.reshape(1, count), held_rows)
    left = lax.ppermute(tail, "feat", to_right)
    right = lax.ppermute(head, "feat", to_left)
    left, own_labels = tie((left, own_labels))
    next_labels = lax.ppermute(own_labels, "dp", flip[2])
    third, second, across_own, left, right, next_labels = tie(
        (third, second, across_own, left, right, next_labels)
    )
    second_outer, second_inner = halves(own_labels, next_labels, second)
    outer = lax.ppermute(second_outer, "dp", flip[1])
    inner = lax.ppermute(second_inner, "dp", flip[1])
    early = early_sums(own_labels, next_labels, train_rows, second)
    early, *sent = tie((early, second, third))
    role = role.reshape(1)
    own_most = stack(role, sent, sent)
    across_most = hop(own_most, (0, 2))
    head, tail = edge_means(own_labels, next_labels, early, third, outer)
    left_means = lax.ppermute(tail, "feat", to_right)
    right_means = lax.ppermute(head, "feat", to_left)
    inner, head, tail = tie((inner, head, tail))
    means, fourth, labels = class_means(own_labels, next_labels, early, third, outer, inner)
    across_last = hop(fourth, (0, 2))
    rows = [train_rows, second, third, fourth]
    near_most = stack(role, rows[:3], [across_own, across_most])
    far_most = hop(near_most, (0, 1), (2, 3))
    most, last = centre(labels, means, rows)
    most, last, means = tie((most, last, means))
    white, score = whiten(
        held_rows, left, right, means, left_means, right_means, held_labels.reshape(1, -1), precision
    )
    score, most = tie((score, most))
    total = gram_most(role, most, near_most, far_most)
    beside = lax.ppermute(score, "feat", flip[1])
    beside, across_last = tie((beside, across_last))
    near_last = stack(role, [fourth], [across_last])
    far_last = hop(near_last, (0, 1), (2, 3))
    scores = [score, beside] + [lax.ppermute(score, "feat", flip[k]) for k in (2, 3)]
    cov, distance = gram_last(
        role, total, last, near_last, far_last, scores, 1.0 / (n * count - C), float(n * width)
    )
    return cov, white, distance.reshape(-1)


def solution(mesh):
    fits = mesh.shape["dp"] == 4 and mesh.shape["feat"] == 4
    return jax.shard_map(
        four_by_four if fits else body,
        mesh=mesh,
        in_specs=(
            P(("layer", "dp"), "feat"),
            P(("layer", "dp"), None),
            P(("layer", "dp"), "feat"),
            P(("layer", "dp")),
            P("layer", "feat", None),
        ),
        out_specs=(P(("layer", "feat"), "dp"), P(("layer", "dp"), "feat"), P(("layer", "dp"))),
        check_vma=False,
    )
```

```python
import jax
import jax.numpy as jnp
from jax import lax
from jax.experimental import pallas as pl
from jax.experimental.pallas import tpu as pltpu
from jax.sharding import PartitionSpec as P

C = 256
BLK = 256
LONG = 10**11
EXTRA = 16
TILE = 128
F32 = jnp.float32
BF16 = jnp.bfloat16
VMEM = pl.BlockSpec(memory_space=pltpu.VMEM)
SMEM = pl.BlockSpec(memory_space=pltpu.SMEM)
ANY = pl.BlockSpec(memory_space=pl.ANY)
HBM = pl.BlockSpec(memory_space=pltpu.HBM)
SMALL = pltpu.CompilerParams(vmem_limit_bytes=8 * 1024 * 1024)
MEDIUM = pltpu.CompilerParams(vmem_limit_bytes=20 * 1024 * 1024)
LARGE = pltpu.CompilerParams(vmem_limit_bytes=24 * 1024 * 1024)


def padded(cells, sides, width):
    for axis, dim in sides:
        count = lax.axis_size(axis)
        ends = count - 1
        head = lax.slice_in_dim(cells, 0, width, axis=dim)
        tail = lax.slice_in_dim(cells, cells.shape[dim] - width, cells.shape[dim], axis=dim)
        cells = jnp.concatenate(
            [
                lax.ppermute(tail, axis, [(i, (i + 1) % count) for i in range(ends)]),
                cells,
                lax.ppermute(head, axis, [((i + 1) % count, i) for i in range(ends)]),
            ],
            axis=dim,
        )
    return cells


def contract_rows(left, right):
    return lax.dot_general(
        left, right, (((0,), (0,)), ((), ())), preferred_element_type=F32
    )


def contract_columns(left, right):
    return lax.dot_general(
        left, right, (((1,), (1,)), ((), ())), preferred_element_type=F32
    )


def body(train_rows, train_labels, held_rows, held_labels, precision):
    local = train_rows.shape[1]
    full = lax.all_gather(train_rows, "feat", axis=1, tiled=True)
    width = full.shape[1]
    classes = jnp.arange(C, dtype=jnp.int32)
    onehot_train = (train_labels == classes[None, :]).astype(BF16)
    local_sums = contract_rows(onehot_train, full)
    local_counts = jnp.sum(onehot_train.astype(F32), axis=0)
    sums, counts = lax.psum((local_sums, local_counts), "dp")
    means = sums / counts[:, None]
    feat_index = lax.axis_index("feat")
    dp_index = lax.axis_index("dp")
    dp_count = lax.axis_size("dp")
    ncols = width // dp_count
    block = lax.psum_scatter(
        contract_rows(full, train_rows), "dp", scatter_dimension=0, tiled=True
    ).T
    sums_rows = lax.dynamic_slice_in_dim(sums, feat_index * local, local, 1)
    means_cols = lax.dynamic_slice_in_dim(means, dp_index * ncols, ncols, 1)
    correction = lax.dot_general(
        sums_rows,
        means_cols,
        (((0,), (0,)), ((), ())),
        precision=lax.Precision.HIGHEST,
        preferred_element_type=F32,
    )
    denominator = float(train_rows.shape[0] * dp_count - C)
    pooled_cov = (block - correction) / denominator
    means_local = lax.dynamic_slice_in_dim(means, feat_index * local, local, 1)
    picked = means_local[held_labels]
    centred = held_rows.astype(F32) - picked
    extended = padded(centred, (("feat", 1),), BLK)
    held_count = held_rows.shape[0]
    nlocal = local // BLK
    windows = extended.reshape(held_count, nlocal + 2, BLK)
    bands = precision.astype(F32).reshape(3, nlocal, BLK, BLK)
    image = jnp.zeros((held_count, nlocal, BLK), F32)
    for k in range(3):
        image = image + jnp.einsum(
            "rmj,mij->rmi",
            windows[:, k : k + nlocal],
            bands[k],
            precision=lax.Precision.HIGHEST,
            preferred_element_type=F32,
        )
    image = image.reshape(held_count, local)
    partial_score = jnp.sum(centred * image, axis=1)
    distance = lax.psum(partial_score, "feat") / width
    return (pooled_cov, image.astype(BF16), distance)


def split3(value):
    high = value.astype(BF16)
    rest = value - high.astype(F32)
    middle = rest.astype(BF16)
    return high, middle, (rest - middle.astype(F32)).astype(BF16)


def onehot_rows(labels):
    classes = lax.broadcasted_iota(jnp.int32, (C, labels.shape[1]), 0)
    return (classes.astype(F32) == labels.astype(F32)).astype(F32)


def cost(flops):
    return pl.CostEstimate(flops=flops, bytes_accessed=0, transcendentals=0)


def class_sums(label_refs, row_refs, columns):
    total = None
    counts = None
    for label_ref, row_ref in zip(label_refs, row_refs, strict=True):
        onehot = onehot_rows(label_ref[...])
        part = jnp.dot(onehot.astype(BF16), row_ref[:, columns], preferred_element_type=F32)
        number = jnp.sum(onehot, axis=1, keepdims=True)
        total = part if total is None else total + part
        counts = number if counts is None else counts + number
    return total, counts


def fetch(sem, *pairs):
    copies = [
        pltpu.make_async_copy(source, target, sem.at[k]) for k, (source, target) in enumerate(pairs)
    ]
    for copy in copies:
        copy.start()
    return copies


def wait(copies):
    for copy in copies:
        copy.wait()


def edges_of(place_ref, first, last, near, far, sem):
    @pl.when(place_ref[0] // 4 % 2 == 0)
    def _():
        wait(fetch(sem, (last, near), (first, far)))

    @pl.when(place_ref[0] // 4 % 2 != 0)
    def _():
        wait(fetch(sem, (first, near), (last, far)))


def outgoing_kernel(place_ref, labels_ref, held_ref, labels_out, near_ref, far_ref, sem, edge_sem):
    width = held_ref.shape[1]
    copies = fetch(sem, (labels_ref, labels_out))
    first = held_ref.at[:, pl.ds(0, BLK)]
    last = held_ref.at[:, pl.ds(width - BLK, BLK)]
    edges_of(place_ref, first, last, near_ref, far_ref, edge_sem)
    wait(copies)


def outgoing(place, labels, held):
    edge = jax.ShapeDtypeStruct((held.shape[0], BLK), BF16)
    return pl.pallas_call(
        outgoing_kernel,
        out_shape=(jax.ShapeDtypeStruct(labels.shape, labels.dtype), edge, edge),
        in_specs=[SMEM] + [HBM] * 2,
        out_specs=(VMEM,) * 3,
        scratch_shapes=[pltpu.SemaphoreType.DMA((1,)), pltpu.SemaphoreType.DMA((2,))],
        compiler_params=SMALL,
        cost_estimate=cost(LONG),
        name="outgoing",
    )(place, labels, held)


def halves_kernel(own_ref, next_ref, rows_ref, outer_ref, inner_ref, labels, sem):
    count, width = rows_ref.shape
    copies = fetch(
        sem,
        (own_ref, labels.at[pl.ds(0, 1)]),
        (next_ref, labels.at[pl.ds(1, 1)]),
        (rows_ref.at[:, pl.ds(0, BLK)], outer_ref.at[pl.ds(0, count), pl.ds(0, BLK)]),
        (rows_ref.at[:, pl.ds(width - BLK, BLK)], outer_ref.at[pl.ds(0, count), pl.ds(BLK, BLK)]),
        (rows_ref.at[:, pl.ds(BLK, width - 2 * BLK)], inner_ref),
    )
    wait(copies[:2])
    index = lax.broadcasted_iota(jnp.int32, (EXTRA, count), 0)
    rows = jnp.where(index == 0, labels[0:1], jnp.where(index == 1, labels[1:2], 0))
    outer_ref[count : count + EXTRA, :count] = rows.astype(F32).astype(BF16)
    outer_ref[count : count + EXTRA, count:] = jnp.zeros((EXTRA, 2 * BLK - count), BF16)
    wait(copies[2:])


def halves(own_labels, next_labels, rows):
    count, width = rows.shape
    return pl.pallas_call(
        halves_kernel,
        out_shape=(
            jax.ShapeDtypeStruct((count + EXTRA, 2 * BLK), rows.dtype),
            jax.ShapeDtypeStruct((count, width - 2 * BLK), rows.dtype),
        ),
        in_specs=[HBM] * 3,
        out_specs=(VMEM, VMEM),
        scratch_shapes=[pltpu.VMEM((2, count), jnp.int32), pltpu.SemaphoreType.DMA((5,))],
        compiler_params=SMALL,
        cost_estimate=cost(1),
        name="halves",
    )(own_labels, next_labels, rows)


def early_kernel(own_label, next_label, own_ref, other_ref, sums_ref, labels, own, other, sem):
    width = own_ref.shape[1]
    copies = fetch(
        sem,
        (own_label, labels.at[pl.ds(0, 1)]),
        (next_label, labels.at[pl.ds(1, 1)]),
        (own_ref, own),
        (other_ref, other),
    )
    wait(copies)
    pairs = [labels.at[p : p + 1] for p in range(2)]
    sums, _ = class_sums(pairs, [own, other], slice(0, width))
    sums_ref[...] = sums


def early_sums(own_labels, next_labels, own, other):
    count, width = own.shape
    return pl.pallas_call(
        early_kernel,
        out_shape=jax.ShapeDtypeStruct((C, width), F32),
        in_specs=[HBM] * 4,
        out_specs=VMEM,
        scratch_shapes=[
            pltpu.VMEM((2, count), jnp.int32),
            pltpu.VMEM((count, width), BF16),
            pltpu.VMEM((count, width), BF16),
            pltpu.SemaphoreType.DMA((4,)),
        ],
        compiler_params=SMALL,
        cost_estimate=cost(LONG),
        name="early_sums",
    )(own_labels, next_labels, own, other)


def four_labels(labels, outer):
    count = labels.shape[1]
    late = outer[count : count + EXTRA, :count].astype(F32)
    return labels[0:1].astype(F32), labels[1:2].astype(F32), late[0:1], late[1:2]


def edges_kernel(place_ref, own_ref, next_ref, early_ref, third_ref, outer_ref, near_ref, far_ref,
                 labels, third, outer, sem):
    count, width = third_ref.shape
    copies = fetch(
        sem,
        (own_ref, labels.at[pl.ds(0, 1)]),
        (next_ref, labels.at[pl.ds(1, 1)]),
        (outer_ref, outer),
        (third_ref.at[:, pl.ds(0, BLK)], third.at[:, pl.ds(0, BLK)]),
        (third_ref.at[:, pl.ds(width - BLK, BLK)], third.at[:, pl.ds(BLK, BLK)]),
    )
    wait(copies[:3])
    hots = [onehot_rows(label) for label in four_labels(labels, outer)]
    counts = sum(jnp.sum(hot, axis=1, keepdims=True) for hot in hots)
    late = jnp.dot(hots[3].astype(BF16), outer[:count, :], preferred_element_type=F32)
    wait(copies[3:])
    late = late + jnp.dot(hots[2].astype(BF16), third[...], preferred_element_type=F32)
    first = (early_ref[:, :BLK] + late[:, :BLK]) / counts
    last = (early_ref[:, width - BLK :] + late[:, BLK:]) / counts

    @pl.when(place_ref[0] // 4 % 2 == 0)
    def _():
        near_ref[...] = last
        far_ref[...] = first

    @pl.when(place_ref[0] // 4 % 2 != 0)
    def _():
        near_ref[...] = first
        far_ref[...] = last


def edge_means(place, own_labels, next_labels, early, third, outer):
    edge = jax.ShapeDtypeStruct((C, BLK), F32)
    count = third.shape[0]
    return pl.pallas_call(
        edges_kernel,
        out_shape=(edge, edge),
        in_specs=[SMEM, HBM, HBM, VMEM, HBM, HBM],
        out_specs=(VMEM, VMEM),
        scratch_shapes=[
            pltpu.VMEM((2, count), jnp.int32),
            pltpu.VMEM((count, 2 * BLK), BF16),
            pltpu.VMEM(outer.shape, BF16),
            pltpu.SemaphoreType.DMA((5,)),
        ],
        compiler_params=SMALL,
        cost_estimate=cost(1),
        name="edge_means",
    )(place, own_labels, next_labels, early, third, outer)


def means_kernel(own_ref, next_ref, early_ref, third_ref, outer_ref, inner_ref,
                 means_ref, fourth_ref, labels_ref, labels, third, outer, inner, sem):
    count, width = third_ref.shape
    wait(
        fetch(
            sem,
            (own_ref, labels.at[pl.ds(0, 1)]),
            (next_ref, labels.at[pl.ds(1, 1)]),
            (third_ref, third),
            (outer_ref, outer),
            (inner_ref, inner),
        )
    )
    groups = four_labels(labels, outer)
    hots = [onehot_rows(label) for label in groups]
    counts = sum(jnp.sum(hot, axis=1, keepdims=True) for hot in hots)
    fourth = jnp.concatenate([outer[:count, :BLK], inner[...], outer[:count, BLK:]], axis=1)
    fourth_ref[...] = fourth
    sums = early_ref[...] + jnp.dot(hots[2].astype(BF16), third[...], preferred_element_type=F32)
    sums = sums + jnp.dot(hots[3].astype(BF16), fourth, preferred_element_type=F32)
    means_ref[...] = sums / counts
    for p, label in enumerate(groups):
        labels_ref[p : p + 1, :] = label


def class_means(own_labels, next_labels, early, third, outer, inner):
    whole = jax.ShapeDtypeStruct(early.shape, F32)
    count = third.shape[0]
    return pl.pallas_call(
        means_kernel,
        out_shape=(
            whole,
            jax.ShapeDtypeStruct(third.shape, third.dtype),
            jax.ShapeDtypeStruct((4, count), F32),
        ),
        in_specs=[HBM, HBM, VMEM, HBM, HBM, HBM],
        out_specs=(VMEM,) * 3,
        scratch_shapes=[
            pltpu.VMEM((2, count), jnp.int32),
            pltpu.VMEM(third.shape, BF16),
            pltpu.VMEM(outer.shape, BF16),
            pltpu.VMEM(inner.shape, BF16),
            pltpu.SemaphoreType.DMA((5,)),
        ],
        compiler_params=MEDIUM,
        cost_estimate=cost(LONG),
        name="class_means",
    )(own_labels, next_labels, early, third, outer, inner)


def stack_kernel(groups, role_ref, *refs):
    *sources, out_ref, sem = refs
    groups = (sources[: groups[0]], sources[groups[0] :])

    def pairs(group):
        start = 0
        for ref in group:
            yield ref, out_ref.at[pl.ds(start, ref.shape[0])]
            start += ref.shape[0]

    for owner, group in zip((True, False), groups, strict=True):

        @pl.when((role_ref[0] % 4 == 0) == owner)
        def _():
            wait(fetch(sem, *pairs(group)))


def stack(role, own, other):
    rows = sum(array.shape[0] for array in own)
    groups = (len(own), len(other))
    return pl.pallas_call(
        lambda *refs: stack_kernel(groups, *refs),
        out_shape=jax.ShapeDtypeStruct((rows, own[0].shape[1]), own[0].dtype),
        in_specs=[SMEM] + [ANY] * sum(groups),
        out_specs=ANY,
        scratch_shapes=[pltpu.SemaphoreType.DMA((max(groups),))],
        compiler_params=SMALL,
        cost_estimate=cost(1),
        name="stack",
    )(role, *own, *other)


def white_kernel(place_ref, held_ref, near_ref, far_ref, means_ref, near_means, far_means,
                 held_labels, precision, white_ref, score_ref, bands, held, means):
    width = held_ref.shape[1]
    for k in range(3):
        bands[:, k * BLK : (k + 1) * BLK] = precision[k]
    held[:, BLK : BLK + width] = held_ref[...]
    means[:, BLK : BLK + width] = means_ref[...]
    sides = (slice(0, BLK), slice(BLK + width, 2 * BLK + width))
    for odd, (far_side, near_side) in enumerate((sides, sides[::-1])):

        @pl.when(place_ref[0] // 4 % 2 == odd)
        def _():
            held[:, near_side] = near_ref[...]
            means[:, near_side] = near_means[...]

        @pl.when(place_ref[0] // 4 == odd)
        def _():
            held[:, far_side] = far_ref[...]
            means[:, far_side] = far_means[...]

        @pl.when(place_ref[0] // 4 == odd + 2)
        def _():
            held[:, far_side] = jnp.zeros(far_ref.shape, BF16)
            means[:, far_side] = jnp.zeros(far_means.shape, F32)

    onehot = onehot_rows(held_labels[...]).astype(BF16)
    picked = sum(contract_rows(onehot, piece) for piece in split3(means[...]))
    centred = held[...].astype(F32) - picked
    pieces = split3(centred)[:2]
    score = jnp.zeros((held_ref.shape[0], 128), F32)
    for m in range(width // BLK):
        inside = slice(m * BLK, (m + 1) * BLK)
        window = slice(m * BLK, (m + 3) * BLK)
        band = bands[inside, :]
        image = sum(contract_columns(piece[:, window], band) for piece in reversed(pieces))
        white_ref[:, inside] = image.astype(BF16)
        product = centred[:, (m + 1) * BLK : (m + 2) * BLK] * image
        for lanes in range(0, BLK, 128):
            score = score + product[:, lanes : lanes + 128]
    score_ref[...] = jnp.sum(score.T, axis=0, keepdims=True)


def whiten(place, held, near, far, means, near_means, far_means, held_labels, precision):
    count, width = held.shape
    return pl.pallas_call(
        white_kernel,
        out_shape=(
            jax.ShapeDtypeStruct((count, width), BF16),
            jax.ShapeDtypeStruct((1, count), F32),
        ),
        in_specs=[SMEM] + [VMEM] * 8,
        out_specs=(VMEM, VMEM),
        scratch_shapes=[
            pltpu.VMEM((width, 3 * BLK), BF16),
            pltpu.VMEM((count, width + 2 * BLK), BF16),
            pltpu.VMEM((C, width + 2 * BLK), F32),
        ],
        compiler_params=MEDIUM,
        cost_estimate=cost(LONG),
        name="whiten",
    )(place, held, near, far, means, near_means, far_means, held_labels, precision)


def choose(role_ref, sem, near, far, target):
    here = role_ref[0] % 2 == 0

    @pl.when(here)
    def _():
        fetch(sem, (near, target))

    @pl.when(jnp.logical_not(here))
    def _():
        fetch(sem, (far, target))

    return pltpu.make_async_copy(near, target, sem.at[0])


def centre_kernel(labels_ref, means_ref, *refs):
    *rows, most_ref, last_ref = refs
    count = rows[0].shape[0]
    most = most_ref.shape[0] // 2
    pieces = split3(means_ref[...])
    for p, ref in enumerate(rows):
        onehot = onehot_rows(labels_ref[p : p + 1]).astype(BF16)
        centred = ref[...].astype(F32) - sum(contract_rows(onehot, piece) for piece in pieces)
        high = centred.astype(BF16)
        low = (centred - high.astype(F32)).astype(BF16)
        into, first, second = (most_ref, p * count, most + p * count)
        if p == len(rows) - 1:
            into, first, second = (last_ref, 0, count)
        into[first : first + count, :] = high
        into[second : second + count, :] = low


def centre(labels, means, rows):
    count, width = rows[0].shape
    return pl.pallas_call(
        centre_kernel,
        out_shape=(
            jax.ShapeDtypeStruct((2 * (len(rows) - 1) * count, width), BF16),
            jax.ShapeDtypeStruct((2 * count, width), BF16),
        ),
        in_specs=[VMEM] * (2 + len(rows)),
        out_specs=(VMEM, VMEM),
        compiler_params=MEDIUM,
        cost_estimate=cost(1),
        name="centre",
    )(labels, means, *rows)


def most_kernel(role_ref, left, near, far, total_ref, right, sem):
    most, width = near.shape
    choose(role_ref, sem, near, far, right).wait()
    for t in range(0, width, BLK):
        high = contract_rows(left[:most, t : t + BLK], right[...])
        total_ref[t : t + BLK, :] = high + contract_rows(left[most:, t : t + BLK], right[...])


def gram_most(role, centred, near, far):
    width = near.shape[1]
    return pl.pallas_call(
        most_kernel,
        out_shape=jax.ShapeDtypeStruct((width, width), F32),
        in_specs=[SMEM, VMEM, ANY, ANY],
        out_specs=VMEM,
        scratch_shapes=[pltpu.VMEM(near.shape, BF16), pltpu.SemaphoreType.DMA((1,))],
        compiler_params=MEDIUM,
        cost_estimate=cost(LONG),
        name="gram_most",
    )(role, centred, near, far)


def last_kernel(scale, features, role_ref, total_ref, last_ref, near, far, own, *refs):
    *others, out_ref, distance_ref, right, tiles, sem, out_sem = refs
    count, width = near.shape
    arrival = choose(role_ref, sem, near, far, right)
    beside, across, beyond = [ref[...] for ref in others]
    distance_ref[...] = ((own[...] + beside) + (across + beyond)) / features
    arrival.wait()
    stores = []
    for k, t in enumerate(range(0, width, TILE)):
        part = contract_rows(last_ref[:count, t : t + TILE], right[...])
        part = part + contract_rows(last_ref[count:, t : t + TILE], right[...])
        tiles[t : t + TILE, :] = (total_ref[t : t + TILE, :] + part) * scale
        stores.append(
            pltpu.make_async_copy(
                tiles.at[pl.ds(t, TILE)], out_ref.at[pl.ds(t, TILE)], out_sem.at[k]
            )
        )
        stores[-1].start()
    wait(stores)


def gram_last(role, total, last, near, far, scores, scale, features):
    count, width = near.shape
    return pl.pallas_call(
        lambda *refs: last_kernel(scale, features, *refs),
        out_shape=(
            jax.ShapeDtypeStruct((width, width), F32),
            jax.ShapeDtypeStruct(scores[0].shape, F32),
        ),
        in_specs=[SMEM, VMEM, VMEM, ANY, ANY] + [VMEM] * len(scores),
        out_specs=(HBM, VMEM),
        scratch_shapes=[
            pltpu.VMEM((count, width), BF16),
            pltpu.VMEM((width, width), F32),
            pltpu.SemaphoreType.DMA((1,)),
            pltpu.SemaphoreType.DMA((width // TILE,)),
        ],
        compiler_params=MEDIUM,
        cost_estimate=cost(LONG),
        name="gram_last",
    )(role, total, last, near, far, *scores)


def four_by_four(train_rows, train_labels, held_rows, held_labels, precision):
    count, width = train_rows.shape
    n = 4
    tie = lax.optimization_barrier
    flip = {k: [(i, i ^ k) for i in range(n)] for k in (1, 2, 3)}
    inward = [(1, 2), (2, 1)]
    feat = lax.axis_index("feat")
    at_end = (feat == 0) | (feat == n - 1)
    role = (lax.axis_index("dp") ^ feat) + n * (feat % 2) + 2 * n * at_end.astype(jnp.int32)
    role = role.astype(jnp.int32).reshape(1)

    def hop(array, *moves):
        pairs = [(d * n + (d ^ s), d * n + (d ^ e)) for d in range(n) for s, e in moves]
        return lax.ppermute(array, ("dp", "feat"), pairs)

    across_own = hop(train_rows, (0, 2))
    third = lax.ppermute(train_rows, "dp", flip[1])
    second = lax.ppermute(train_rows, "dp", flip[2])
    own_labels, near, far = outgoing(role, train_labels.reshape(1, count), held_rows)
    near = lax.ppermute(near, "feat", flip[1])
    far = lax.ppermute(far, "feat", flip[3])
    near, own_labels = tie((near, own_labels))
    next_labels = lax.ppermute(own_labels, "dp", flip[2])
    third, second, across_own, near, far, next_labels = tie(
        (third, second, across_own, near, far, next_labels)
    )
    second_outer, second_inner = halves(own_labels, next_labels, second)
    outer = lax.ppermute(second_outer, "dp", flip[1])
    inner = lax.ppermute(second_inner, "dp", flip[1])
    early = early_sums(own_labels, next_labels, train_rows, second)
    early, *sent = tie((early, second, third))
    own_most = stack(role, sent, sent)
    across_most = hop(own_most, (0, 2))
    near_edge, far_edge = edge_means(role, own_labels, next_labels, early, third, outer)
    near_means = lax.ppermute(near_edge, "feat", flip[1])
    far_means = lax.ppermute(far_edge, "feat", inward)
    inner, near_edge = tie((inner, near_edge))
    means, fourth, labels = class_means(own_labels, next_labels, early, third, outer, inner)
    across_last = hop(fourth, (0, 2))
    rows = [train_rows, second, third, fourth]
    near_most = stack(role, rows[:3], [across_own, across_most])
    far_most = lax.ppermute(near_most, "feat", flip[1])
    most, last = centre(labels, means, rows)
    most, last, means = tie((most, last, means))
    white, score = whiten(
        role, held_rows, near, far, means, near_means, far_means, held_labels.reshape(1, -1), precision
    )
    score, most = tie((score, most))
    total = gram_most(role, most, near_most, far_most)
    beside = lax.ppermute(score, "feat", flip[1])
    beside, across_last = tie((beside, across_last))
    near_last = stack(role, [fourth], [across_last])
    far_last = lax.ppermute(near_last, "feat", flip[1])
    scores = [score, beside] + [lax.ppermute(score, "feat", flip[k]) for k in (2, 3)]
    cov, distance = gram_last(
        role, total, last, near_last, far_last, scores, 1.0 / (n * count - C), float(n * width)
    )
    return cov, white, distance.reshape(-1)


def solution(mesh):
    fits = mesh.shape["dp"] == 4 and mesh.shape["feat"] == 4
    return jax.shard_map(
        four_by_four if fits else body,
        mesh=mesh,
        in_specs=(
            P(("layer", "dp"), "feat"),
            P(("layer", "dp"), None),
            P(("layer", "dp"), "feat"),
            P(("layer", "dp")),
            P("layer", "feat", None),
        ),
        out_specs=(P(("layer", "feat"), "dp"), P(("layer", "dp"), "feat"), P(("layer", "dp"))),
        check_vma=False,
    )
```

```python
import jax
import jax.numpy as jnp
from jax import lax
from jax.experimental import pallas as pl
from jax.experimental.pallas import tpu as pltpu
from jax.sharding import PartitionSpec as P

C = 256
BLK = 256
LONG = 10**11
EXTRA = 16
TILE = 128
F32 = jnp.float32
BF16 = jnp.bfloat16
VMEM = pl.BlockSpec(memory_space=pltpu.VMEM)
SMEM = pl.BlockSpec(memory_space=pltpu.SMEM)
ANY = pl.BlockSpec(memory_space=pl.ANY)
HBM = pl.BlockSpec(memory_space=pltpu.HBM)
SMALL = pltpu.CompilerParams(vmem_limit_bytes=8 * 1024 * 1024)
MEDIUM = pltpu.CompilerParams(vmem_limit_bytes=20 * 1024 * 1024)
MIDDLE = pltpu.CompilerParams(vmem_limit_bytes=12 * 1024 * 1024)


def padded(cells, sides, width):
    for axis, dim in sides:
        count = lax.axis_size(axis)
        ends = count - 1
        head = lax.slice_in_dim(cells, 0, width, axis=dim)
        tail = lax.slice_in_dim(cells, cells.shape[dim] - width, cells.shape[dim], axis=dim)
        cells = jnp.concatenate(
            [
                lax.ppermute(tail, axis, [(i, (i + 1) % count) for i in range(ends)]),
                cells,
                lax.ppermute(head, axis, [((i + 1) % count, i) for i in range(ends)]),
            ],
            axis=dim,
        )
    return cells


def contract_rows(left, right):
    return lax.dot_general(
        left, right, (((0,), (0,)), ((), ())), preferred_element_type=F32
    )


def contract_columns(left, right):
    return lax.dot_general(
        left, right, (((1,), (1,)), ((), ())), preferred_element_type=F32
    )


def body(train_rows, train_labels, held_rows, held_labels, precision):
    local = train_rows.shape[1]
    full = lax.all_gather(train_rows, "feat", axis=1, tiled=True)
    width = full.shape[1]
    classes = jnp.arange(C, dtype=jnp.int32)
    onehot_train = (train_labels == classes[None, :]).astype(BF16)
    local_sums = contract_rows(onehot_train, full)
    local_counts = jnp.sum(onehot_train.astype(F32), axis=0)
    sums, counts = lax.psum((local_sums, local_counts), "dp")
    means = sums / counts[:, None]
    feat_index = lax.axis_index("feat")
    dp_index = lax.axis_index("dp")
    dp_count = lax.axis_size("dp")
    ncols = width // dp_count
    block = lax.psum_scatter(
        contract_rows(full, train_rows), "dp", scatter_dimension=0, tiled=True
    ).T
    sums_rows = lax.dynamic_slice_in_dim(sums, feat_index * local, local, 1)
    means_cols = lax.dynamic_slice_in_dim(means, dp_index * ncols, ncols, 1)
    correction = lax.dot_general(
        sums_rows,
        means_cols,
        (((0,), (0,)), ((), ())),
        precision=lax.Precision.HIGHEST,
        preferred_element_type=F32,
    )
    denominator = float(train_rows.shape[0] * dp_count - C)
    pooled_cov = (block - correction) / denominator
    means_local = lax.dynamic_slice_in_dim(means, feat_index * local, local, 1)
    picked = means_local[held_labels]
    centred = held_rows.astype(F32) - picked
    extended = padded(centred, (("feat", 1),), BLK)
    held_count = held_rows.shape[0]
    nlocal = local // BLK
    windows = extended.reshape(held_count, nlocal + 2, BLK)
    bands = precision.astype(F32).reshape(3, nlocal, BLK, BLK)
    image = jnp.zeros((held_count, nlocal, BLK), F32)
    for k in range(3):
        image = image + jnp.einsum(
            "rmj,mij->rmi",
            windows[:, k : k + nlocal],
            bands[k],
            precision=lax.Precision.HIGHEST,
            preferred_element_type=F32,
        )
    image = image.reshape(held_count, local)
    partial_score = jnp.sum(centred * image, axis=1)
    distance = lax.psum(partial_score, "feat") / width
    return (pooled_cov, image.astype(BF16), distance)


def split3(value):
    high = value.astype(BF16)
    rest = value - high.astype(F32)
    middle = rest.astype(BF16)
    return high, middle, (rest - middle.astype(F32)).astype(BF16)


def onehot_rows(labels):
    classes = lax.broadcasted_iota(jnp.int32, (C, labels.shape[1]), 0)
    return (classes.astype(F32) == labels.astype(F32)).astype(F32)


def cost(flops):
    return pl.CostEstimate(flops=flops, bytes_accessed=0, transcendentals=0)


def class_sums(label_refs, row_refs, columns):
    total = None
    counts = None
    for label_ref, row_ref in zip(label_refs, row_refs, strict=True):
        onehot = onehot_rows(label_ref[...])
        part = jnp.dot(onehot.astype(BF16), row_ref[:, columns], preferred_element_type=F32)
        number = jnp.sum(onehot, axis=1, keepdims=True)
        total = part if total is None else total + part
        counts = number if counts is None else counts + number
    return total, counts


def fetch(sem, *pairs):
    copies = [
        pltpu.make_async_copy(source, target, sem.at[k]) for k, (source, target) in enumerate(pairs)
    ]
    for copy in copies:
        copy.start()
    return copies


def wait(copies):
    for copy in copies:
        copy.wait()


def edges_of(place_ref, first, last, near, far, sem):
    @pl.when(place_ref[0] // 4 % 2 == 0)
    def _():
        wait(fetch(sem, (last, near), (first, far)))

    @pl.when(place_ref[0] // 4 % 2 != 0)
    def _():
        wait(fetch(sem, (first, near), (last, far)))


def outgoing_kernel(place_ref, labels_ref, held_ref, labels_out, near_ref, far_ref, sem, edge_sem):
    width = held_ref.shape[1]
    copies = fetch(sem, (labels_ref, labels_out))
    first = held_ref.at[:, pl.ds(0, BLK)]
    last = held_ref.at[:, pl.ds(width - BLK, BLK)]
    edges_of(place_ref, first, last, near_ref, far_ref, edge_sem)
    wait(copies)


def outgoing(place, labels, held):
    edge = jax.ShapeDtypeStruct((held.shape[0], BLK), BF16)
    return pl.pallas_call(
        outgoing_kernel,
        out_shape=(jax.ShapeDtypeStruct(labels.shape, labels.dtype), edge, edge),
        in_specs=[SMEM] + [HBM] * 2,
        out_specs=(VMEM,) * 3,
        scratch_shapes=[pltpu.SemaphoreType.DMA((1,)), pltpu.SemaphoreType.DMA((2,))],
        compiler_params=SMALL,
        cost_estimate=cost(LONG),
        name="outgoing",
    )(place, labels, held)


def halves_kernel(own_ref, next_ref, rows_ref, outer_ref, inner_ref, labels, sem):
    count, width = rows_ref.shape
    copies = fetch(
        sem,
        (own_ref, labels.at[pl.ds(0, 1)]),
        (next_ref, labels.at[pl.ds(1, 1)]),
        (rows_ref.at[:, pl.ds(0, BLK)], outer_ref.at[pl.ds(0, count), pl.ds(0, BLK)]),
        (rows_ref.at[:, pl.ds(width - BLK, BLK)], outer_ref.at[pl.ds(0, count), pl.ds(BLK, BLK)]),
        (rows_ref.at[:, pl.ds(BLK, width - 2 * BLK)], inner_ref),
    )
    wait(copies[:2])
    index = lax.broadcasted_iota(jnp.int32, (EXTRA, count), 0)
    rows = jnp.where(index == 0, labels[0:1], jnp.where(index == 1, labels[1:2], 0))
    outer_ref[count : count + EXTRA, :count] = rows.astype(F32).astype(BF16)
    outer_ref[count : count + EXTRA, count:] = jnp.zeros((EXTRA, 2 * BLK - count), BF16)
    wait(copies[2:])


def halves(own_labels, next_labels, rows):
    count, width = rows.shape
    return pl.pallas_call(
        halves_kernel,
        out_shape=(
            jax.ShapeDtypeStruct((count + EXTRA, 2 * BLK), rows.dtype),
            jax.ShapeDtypeStruct((count, width - 2 * BLK), rows.dtype),
        ),
        in_specs=[HBM] * 3,
        out_specs=(VMEM, VMEM),
        scratch_shapes=[pltpu.VMEM((2, count), jnp.int32), pltpu.SemaphoreType.DMA((5,))],
        compiler_params=SMALL,
        cost_estimate=cost(1),
        name="halves",
    )(own_labels, next_labels, rows)


def early_kernel(own_label, next_label, own_ref, other_ref, sums_ref, labels, own, other, sem):
    width = own_ref.shape[1]
    copies = fetch(
        sem,
        (own_label, labels.at[pl.ds(0, 1)]),
        (next_label, labels.at[pl.ds(1, 1)]),
        (own_ref, own),
        (other_ref, other),
    )
    wait(copies)
    pairs = [labels.at[p : p + 1] for p in range(2)]
    sums, _ = class_sums(pairs, [own, other], slice(0, width))
    sums_ref[...] = sums


def early_sums(own_labels, next_labels, own, other):
    count, width = own.shape
    return pl.pallas_call(
        early_kernel,
        out_shape=jax.ShapeDtypeStruct((C, width), F32),
        in_specs=[HBM] * 4,
        out_specs=VMEM,
        scratch_shapes=[
            pltpu.VMEM((2, count), jnp.int32),
            pltpu.VMEM((count, width), BF16),
            pltpu.VMEM((count, width), BF16),
            pltpu.SemaphoreType.DMA((4,)),
        ],
        compiler_params=SMALL,
        cost_estimate=cost(LONG),
        name="early_sums",
    )(own_labels, next_labels, own, other)


def four_labels(labels, outer):
    count = labels.shape[1]
    late = outer[count : count + EXTRA, :count].astype(F32)
    return labels[0:1].astype(F32), labels[1:2].astype(F32), late[0:1], late[1:2]


def edges_kernel(place_ref, own_ref, next_ref, early_ref, third_ref, outer_ref, near_ref, far_ref,
                 labels, third, outer, sem):
    count, width = third_ref.shape
    copies = fetch(
        sem,
        (own_ref, labels.at[pl.ds(0, 1)]),
        (next_ref, labels.at[pl.ds(1, 1)]),
        (outer_ref, outer),
        (third_ref.at[:, pl.ds(0, BLK)], third.at[:, pl.ds(0, BLK)]),
        (third_ref.at[:, pl.ds(width - BLK, BLK)], third.at[:, pl.ds(BLK, BLK)]),
    )
    wait(copies[:3])
    hots = [onehot_rows(label) for label in four_labels(labels, outer)]
    counts = sum(jnp.sum(hot, axis=1, keepdims=True) for hot in hots)
    late = jnp.dot(hots[3].astype(BF16), outer[:count, :], preferred_element_type=F32)
    wait(copies[3:])
    late = late + jnp.dot(hots[2].astype(BF16), third[...], preferred_element_type=F32)
    first = (early_ref[:, :BLK] + late[:, :BLK]) / counts
    last = (early_ref[:, width - BLK :] + late[:, BLK:]) / counts

    @pl.when(place_ref[0] // 4 % 2 == 0)
    def _():
        near_ref[...] = last
        far_ref[...] = first

    @pl.when(place_ref[0] // 4 % 2 != 0)
    def _():
        near_ref[...] = first
        far_ref[...] = last


def edge_means(place, own_labels, next_labels, early, third, outer):
    edge = jax.ShapeDtypeStruct((C, BLK), F32)
    count = third.shape[0]
    return pl.pallas_call(
        edges_kernel,
        out_shape=(edge, edge),
        in_specs=[SMEM, HBM, HBM, VMEM, HBM, HBM],
        out_specs=(VMEM, VMEM),
        scratch_shapes=[
            pltpu.VMEM((2, count), jnp.int32),
            pltpu.VMEM((count, 2 * BLK), BF16),
            pltpu.VMEM(outer.shape, BF16),
            pltpu.SemaphoreType.DMA((5,)),
        ],
        compiler_params=SMALL,
        cost_estimate=cost(1),
        name="edge_means",
    )(place, own_labels, next_labels, early, third, outer)


def means_kernel(own_ref, next_ref, early_ref, third_ref, outer_ref, inner_ref,
                 means_ref, fourth_ref, labels_ref, labels, third, outer, inner, sem):
    count, width = third_ref.shape
    wait(
        fetch(
            sem,
            (own_ref, labels.at[pl.ds(0, 1)]),
            (next_ref, labels.at[pl.ds(1, 1)]),
            (third_ref, third),
            (outer_ref, outer),
            (inner_ref, inner),
        )
    )
    groups = four_labels(labels, outer)
    hots = [onehot_rows(label) for label in groups]
    counts = sum(jnp.sum(hot, axis=1, keepdims=True) for hot in hots)
    fourth = jnp.concatenate([outer[:count, :BLK], inner[...], outer[:count, BLK:]], axis=1)
    fourth_ref[...] = fourth
    sums = early_ref[...] + jnp.dot(hots[2].astype(BF16), third[...], preferred_element_type=F32)
    sums = sums + jnp.dot(hots[3].astype(BF16), fourth, preferred_element_type=F32)
    means_ref[...] = sums / counts
    for p, label in enumerate(groups):
        labels_ref[p : p + 1, :] = label


def class_means(own_labels, next_labels, early, third, outer, inner):
    whole = jax.ShapeDtypeStruct(early.shape, F32)
    count = third.shape[0]
    return pl.pallas_call(
        means_kernel,
        out_shape=(
            whole,
            jax.ShapeDtypeStruct(third.shape, third.dtype),
            jax.ShapeDtypeStruct((4, count), F32),
        ),
        in_specs=[HBM, HBM, VMEM, HBM, HBM, HBM],
        out_specs=(VMEM,) * 3,
        scratch_shapes=[
            pltpu.VMEM((2, count), jnp.int32),
            pltpu.VMEM(third.shape, BF16),
            pltpu.VMEM(outer.shape, BF16),
            pltpu.VMEM(inner.shape, BF16),
            pltpu.SemaphoreType.DMA((5,)),
        ],
        compiler_params=MIDDLE,
        cost_estimate=cost(LONG),
        name="class_means",
    )(own_labels, next_labels, early, third, outer, inner)


def stack_kernel(groups, role_ref, *refs):
    *sources, out_ref, sem = refs
    groups = (sources[: groups[0]], sources[groups[0] :])

    def pairs(group):
        start = 0
        for ref in group:
            yield ref, out_ref.at[pl.ds(start, ref.shape[0])]
            start += ref.shape[0]

    for owner, group in zip((True, False), groups, strict=True):

        @pl.when((role_ref[0] % 4 == 0) == owner)
        def _():
            wait(fetch(sem, *pairs(group)))


def stack(role, own, other):
    rows = sum(array.shape[0] for array in own)
    groups = (len(own), len(other))
    return pl.pallas_call(
        lambda *refs: stack_kernel(groups, *refs),
        out_shape=jax.ShapeDtypeStruct((rows, own[0].shape[1]), own[0].dtype),
        in_specs=[SMEM] + [ANY] * sum(groups),
        out_specs=ANY,
        scratch_shapes=[pltpu.SemaphoreType.DMA((max(groups),))],
        compiler_params=SMALL,
        cost_estimate=cost(1),
        name="stack",
    )(role, *own, *other)


def white_kernel(place_ref, held_ref, near_ref, far_ref, means_ref, near_means, far_means,
                 held_labels, precision, white_ref, score_ref, bands, held, means):
    width = held_ref.shape[1]
    for k in range(3):
        bands[:, k * BLK : (k + 1) * BLK] = precision[k]
    held[:, BLK : BLK + width] = held_ref[...]
    means[:, BLK : BLK + width] = means_ref[...]
    sides = (slice(0, BLK), slice(BLK + width, 2 * BLK + width))
    for odd, (far_side, near_side) in enumerate((sides, sides[::-1])):

        @pl.when(place_ref[0] // 4 % 2 == odd)
        def _():
            held[:, near_side] = near_ref[...]
            means[:, near_side] = near_means[...]

        @pl.when(place_ref[0] // 4 == odd)
        def _():
            held[:, far_side] = far_ref[...]
            means[:, far_side] = far_means[...]

        @pl.when(place_ref[0] // 4 == odd + 2)
        def _():
            held[:, far_side] = jnp.zeros(far_ref.shape, BF16)
            means[:, far_side] = jnp.zeros(far_means.shape, F32)

    onehot = onehot_rows(held_labels[...]).astype(BF16)
    picked = sum(contract_rows(onehot, piece) for piece in split3(means[...]))
    centred = held[...].astype(F32) - picked
    pieces = split3(centred)[:2]
    score = jnp.zeros((held_ref.shape[0], 128), F32)
    for m in range(width // BLK):
        inside = slice(m * BLK, (m + 1) * BLK)
        window = slice(m * BLK, (m + 3) * BLK)
        band = bands[inside, :]
        image = sum(contract_columns(piece[:, window], band) for piece in reversed(pieces))
        white_ref[:, inside] = image.astype(BF16)
        product = centred[:, (m + 1) * BLK : (m + 2) * BLK] * image
        for lanes in range(0, BLK, 128):
            score = score + product[:, lanes : lanes + 128]
    score_ref[...] = jnp.sum(score.T, axis=0, keepdims=True)


def whiten(place, held, near, far, means, near_means, far_means, held_labels, precision):
    count, width = held.shape
    return pl.pallas_call(
        white_kernel,
        out_shape=(
            jax.ShapeDtypeStruct((count, width), BF16),
            jax.ShapeDtypeStruct((1, count), F32),
        ),
        in_specs=[SMEM] + [VMEM] * 8,
        out_specs=(VMEM, VMEM),
        scratch_shapes=[
            pltpu.VMEM((width, 3 * BLK), BF16),
            pltpu.VMEM((count, width + 2 * BLK), BF16),
            pltpu.VMEM((C, width + 2 * BLK), F32),
        ],
        compiler_params=MEDIUM,
        cost_estimate=cost(LONG),
        name="whiten",
    )(place, held, near, far, means, near_means, far_means, held_labels, precision)


def choose(role_ref, sem, near, far, target):
    here = role_ref[0] % 2 == 0

    @pl.when(here)
    def _():
        fetch(sem, (near, target))

    @pl.when(jnp.logical_not(here))
    def _():
        fetch(sem, (far, target))

    return pltpu.make_async_copy(near, target, sem.at[0])


def centre_kernel(labels_ref, means_ref, *refs):
    *rows, most_ref, last_ref = refs
    count = rows[0].shape[0]
    most = most_ref.shape[0] // 2
    pieces = split3(means_ref[...])
    for p, ref in enumerate(rows):
        onehot = onehot_rows(labels_ref[p : p + 1]).astype(BF16)
        centred = ref[...].astype(F32) - sum(contract_rows(onehot, piece) for piece in pieces)
        high = centred.astype(BF16)
        low = (centred - high.astype(F32)).astype(BF16)
        into, first, second = (most_ref, p * count, most + p * count)
        if p == len(rows) - 1:
            into, first, second = (last_ref, 0, count)
        into[first : first + count, :] = high
        into[second : second + count, :] = low


def centre(labels, means, rows):
    count, width = rows[0].shape
    return pl.pallas_call(
        centre_kernel,
        out_shape=(
            jax.ShapeDtypeStruct((2 * (len(rows) - 1) * count, width), BF16),
            jax.ShapeDtypeStruct((2 * count, width), BF16),
        ),
        in_specs=[VMEM] * (2 + len(rows)),
        out_specs=(VMEM, VMEM),
        compiler_params=MIDDLE,
        cost_estimate=cost(1),
        name="centre",
    )(labels, means, *rows)


def most_kernel(role_ref, left, near, far, total_ref, right, sem):
    most, width = near.shape
    choose(role_ref, sem, near, far, right).wait()
    for t in range(0, width, BLK):
        high = contract_rows(left[:most, t : t + BLK], right[...])
        total_ref[t : t + BLK, :] = high + contract_rows(left[most:, t : t + BLK], right[...])


def gram_most(role, centred, near, far):
    width = near.shape[1]
    return pl.pallas_call(
        most_kernel,
        out_shape=jax.ShapeDtypeStruct((width, width), F32),
        in_specs=[SMEM, VMEM, ANY, ANY],
        out_specs=VMEM,
        scratch_shapes=[pltpu.VMEM(near.shape, BF16), pltpu.SemaphoreType.DMA((1,))],
        compiler_params=MIDDLE,
        cost_estimate=cost(LONG),
        name="gram_most",
    )(role, centred, near, far)


def last_kernel(scale, features, role_ref, total_ref, last_ref, near, far, own, *refs):
    *others, out_ref, distance_ref, right, tiles, sem, out_sem = refs
    count, width = near.shape
    arrival = choose(role_ref, sem, near, far, right)
    beside, across, beyond = [ref[...] for ref in others]
    distance_ref[...] = ((own[...] + beside) + (across + beyond)) / features
    arrival.wait()
    stores = []
    for k, t in enumerate(range(0, width, TILE)):
        part = contract_rows(last_ref[:count, t : t + TILE], right[...])
        part = part + contract_rows(last_ref[count:, t : t + TILE], right[...])
        tiles[t : t + TILE, :] = (total_ref[t : t + TILE, :] + part) * scale
        stores.append(
            pltpu.make_async_copy(
                tiles.at[pl.ds(t, TILE)], out_ref.at[pl.ds(t, TILE)], out_sem.at[k]
            )
        )
        stores[-1].start()
    wait(stores)


def gram_last(role, total, last, near, far, scores, scale, features):
    count, width = near.shape
    return pl.pallas_call(
        lambda *refs: last_kernel(scale, features, *refs),
        out_shape=(
            jax.ShapeDtypeStruct((width, width), F32),
            jax.ShapeDtypeStruct(scores[0].shape, F32),
        ),
        in_specs=[SMEM, VMEM, VMEM, ANY, ANY] + [VMEM] * len(scores),
        out_specs=(HBM, VMEM),
        scratch_shapes=[
            pltpu.VMEM((count, width), BF16),
            pltpu.VMEM((width, width), F32),
            pltpu.SemaphoreType.DMA((1,)),
            pltpu.SemaphoreType.DMA((width // TILE,)),
        ],
        compiler_params=MIDDLE,
        cost_estimate=cost(LONG),
        name="gram_last",
    )(role, total, last, near, far, *scores)


def four_by_four(train_rows, train_labels, held_rows, held_labels, precision):
    count, width = train_rows.shape
    n = 4
    tie = lax.optimization_barrier
    flip = {k: [(i, i ^ k) for i in range(n)] for k in (1, 2, 3)}
    inward = [(1, 2), (2, 1)]
    feat = lax.axis_index("feat")
    at_end = (feat == 0) | (feat == n - 1)
    role = (lax.axis_index("dp") ^ feat) + n * (feat % 2) + 2 * n * at_end.astype(jnp.int32)
    role = role.astype(jnp.int32).reshape(1)

    def hop(array, *moves):
        pairs = [(d * n + (d ^ s), d * n + (d ^ e)) for d in range(n) for s, e in moves]
        return lax.ppermute(array, ("dp", "feat"), pairs)

    across_own = hop(train_rows, (0, 2))
    third = lax.ppermute(train_rows, "dp", flip[1])
    second = lax.ppermute(train_rows, "dp", flip[2])
    own_labels, near, far = outgoing(role, train_labels.reshape(1, count), held_rows)
    near = lax.ppermute(near, "feat", flip[1])
    far = lax.ppermute(far, "feat", flip[3])
    near, own_labels = tie((near, own_labels))
    next_labels = lax.ppermute(own_labels, "dp", flip[2])
    second, third, across_own, near, far, next_labels = tie(
        (second, third, across_own, near, far, next_labels)
    )
    second_outer, second_inner = halves(own_labels, next_labels, second)
    outer = lax.ppermute(second_outer, "dp", flip[1])
    inner = lax.ppermute(second_inner, "dp", flip[1])
    early = early_sums(own_labels, next_labels, train_rows, second)
    early, *sent = tie((early, second, third))
    own_most = stack(role, sent, sent)
    across_most = hop(own_most, (0, 2))
    near_edge, far_edge = edge_means(role, own_labels, next_labels, early, third, outer)
    near_means = lax.ppermute(near_edge, "feat", flip[1])
    far_means = lax.ppermute(far_edge, "feat", inward)
    inner, near_edge = tie((inner, near_edge))
    means, fourth, labels = class_means(own_labels, next_labels, early, third, outer, inner)
    across_last = hop(fourth, (0, 2))
    rows = [train_rows, second, third, fourth]
    near_most = stack(role, rows[:3], [across_own, across_most])
    far_most = lax.ppermute(near_most, "feat", flip[1])
    most, last = centre(labels, means, rows)
    most, last, means = tie((most, last, means))
    white, score = whiten(
        role, held_rows, near, far, means, near_means, far_means, held_labels.reshape(1, -1), precision
    )
    score, most = tie((score, most))
    total = gram_most(role, most, near_most, far_most)
    beside = lax.ppermute(score, "feat", flip[1])
    beside, across_last = tie((beside, across_last))
    near_last = stack(role, [fourth], [across_last])
    far_last = lax.ppermute(near_last, "feat", flip[1])
    scores = [score, beside] + [lax.ppermute(score, "feat", flip[k]) for k in (2, 3)]
    cov, distance = gram_last(
        role, total, last, near_last, far_last, scores, 1.0 / (n * count - C), float(n * width)
    )
    return cov, white, distance.reshape(-1)


def solution(mesh):
    fits = mesh.shape["dp"] == 4 and mesh.shape["feat"] == 4
    return jax.shard_map(
        four_by_four if fits else body,
        mesh=mesh,
        in_specs=(
            P(("layer", "dp"), "feat"),
            P(("layer", "dp"), None),
            P(("layer", "dp"), "feat"),
            P(("layer", "dp")),
            P("layer", "feat", None),
        ),
        out_specs=(P(("layer", "feat"), "dp"), P(("layer", "dp"), "feat"), P(("layer", "dp"))),
        check_vma=False,
    )
```

```python
import jax
import jax.numpy as jnp
from jax import lax
from jax.experimental import pallas as pl
from jax.experimental.pallas import tpu as pltpu
from jax.sharding import PartitionSpec as P

C = 256
BLK = 256
LONG = 10**11
EXTRA = 16
TILE = 128
F32 = jnp.float32
BF16 = jnp.bfloat16
VMEM = pl.BlockSpec(memory_space=pltpu.VMEM)
SMEM = pl.BlockSpec(memory_space=pltpu.SMEM)
ANY = pl.BlockSpec(memory_space=pl.ANY)
HBM = pl.BlockSpec(memory_space=pltpu.HBM)
SMALL = pltpu.CompilerParams(vmem_limit_bytes=8 * 1024 * 1024)
MEDIUM = pltpu.CompilerParams(vmem_limit_bytes=20 * 1024 * 1024)
MIDDLE = pltpu.CompilerParams(vmem_limit_bytes=12 * 1024 * 1024)


def padded(cells, sides, width):
    for axis, dim in sides:
        count = lax.axis_size(axis)
        ends = count - 1
        head = lax.slice_in_dim(cells, 0, width, axis=dim)
        tail = lax.slice_in_dim(cells, cells.shape[dim] - width, cells.shape[dim], axis=dim)
        cells = jnp.concatenate(
            [
                lax.ppermute(tail, axis, [(i, (i + 1) % count) for i in range(ends)]),
                cells,
                lax.ppermute(head, axis, [((i + 1) % count, i) for i in range(ends)]),
            ],
            axis=dim,
        )
    return cells


def contract_rows(left, right):
    return lax.dot_general(
        left, right, (((0,), (0,)), ((), ())), preferred_element_type=F32
    )


def contract_columns(left, right):
    return lax.dot_general(
        left, right, (((1,), (1,)), ((), ())), preferred_element_type=F32
    )


def body(train_rows, train_labels, held_rows, held_labels, precision):
    local = train_rows.shape[1]
    full = lax.all_gather(train_rows, "feat", axis=1, tiled=True)
    width = full.shape[1]
    classes = jnp.arange(C, dtype=jnp.int32)
    onehot_train = (train_labels == classes[None, :]).astype(BF16)
    local_sums = contract_rows(onehot_train, full)
    local_counts = jnp.sum(onehot_train.astype(F32), axis=0)
    sums, counts = lax.psum((local_sums, local_counts), "dp")
    means = sums / counts[:, None]
    feat_index = lax.axis_index("feat")
    dp_index = lax.axis_index("dp")
    dp_count = lax.axis_size("dp")
    ncols = width // dp_count
    block = lax.psum_scatter(
        contract_rows(full, train_rows), "dp", scatter_dimension=0, tiled=True
    ).T
    sums_rows = lax.dynamic_slice_in_dim(sums, feat_index * local, local, 1)
    means_cols = lax.dynamic_slice_in_dim(means, dp_index * ncols, ncols, 1)
    correction = lax.dot_general(
        sums_rows,
        means_cols,
        (((0,), (0,)), ((), ())),
        precision=lax.Precision.HIGHEST,
        preferred_element_type=F32,
    )
    denominator = float(train_rows.shape[0] * dp_count - C)
    pooled_cov = (block - correction) / denominator
    means_local = lax.dynamic_slice_in_dim(means, feat_index * local, local, 1)
    picked = means_local[held_labels]
    centred = held_rows.astype(F32) - picked
    extended = padded(centred, (("feat", 1),), BLK)
    held_count = held_rows.shape[0]
    nlocal = local // BLK
    windows = extended.reshape(held_count, nlocal + 2, BLK)
    bands = precision.astype(F32).reshape(3, nlocal, BLK, BLK)
    image = jnp.zeros((held_count, nlocal, BLK), F32)
    for k in range(3):
        image = image + jnp.einsum(
            "rmj,mij->rmi",
            windows[:, k : k + nlocal],
            bands[k],
            precision=lax.Precision.HIGHEST,
            preferred_element_type=F32,
        )
    image = image.reshape(held_count, local)
    partial_score = jnp.sum(centred * image, axis=1)
    distance = lax.psum(partial_score, "feat") / width
    return (pooled_cov, image.astype(BF16), distance)


def split3(value):
    high = value.astype(BF16)
    rest = value - high.astype(F32)
    middle = rest.astype(BF16)
    return high, middle, (rest - middle.astype(F32)).astype(BF16)


def onehot_rows(labels):
    classes = lax.broadcasted_iota(jnp.int32, (C, labels.shape[1]), 0)
    return (classes.astype(F32) == labels.astype(F32)).astype(F32)


def cost(flops):
    return pl.CostEstimate(flops=flops, bytes_accessed=0, transcendentals=0)


def class_sums(label_refs, row_refs, columns):
    total = None
    counts = None
    for label_ref, row_ref in zip(label_refs, row_refs, strict=True):
        onehot = onehot_rows(label_ref[...])
        part = jnp.dot(onehot.astype(BF16), row_ref[:, columns], preferred_element_type=F32)
        number = jnp.sum(onehot, axis=1, keepdims=True)
        total = part if total is None else total + part
        counts = number if counts is None else counts + number
    return total, counts


def fetch(sem, *pairs):
    copies = [
        pltpu.make_async_copy(source, target, sem.at[k]) for k, (source, target) in enumerate(pairs)
    ]
    for copy in copies:
        copy.start()
    return copies


def wait(copies):
    for copy in copies:
        copy.wait()


def edges_of(place_ref, first, last, near, far, sem):
    @pl.when(place_ref[0] // 4 % 2 == 0)
    def _():
        wait(fetch(sem, (last, near), (first, far)))

    @pl.when(place_ref[0] // 4 % 2 != 0)
    def _():
        wait(fetch(sem, (first, near), (last, far)))


def outgoing_kernel(place_ref, labels_ref, held_ref, labels_out, near_ref, far_ref, sem, edge_sem):
    width = held_ref.shape[1]
    copies = fetch(sem, (labels_ref, labels_out))
    first = held_ref.at[:, pl.ds(0, BLK)]
    last = held_ref.at[:, pl.ds(width - BLK, BLK)]
    edges_of(place_ref, first, last, near_ref, far_ref, edge_sem)
    wait(copies)


def outgoing(place, labels, held):
    edge = jax.ShapeDtypeStruct((held.shape[0], BLK), BF16)
    return pl.pallas_call(
        outgoing_kernel,
        out_shape=(jax.ShapeDtypeStruct(labels.shape, labels.dtype), edge, edge),
        in_specs=[SMEM] + [HBM] * 2,
        out_specs=(VMEM,) * 3,
        scratch_shapes=[pltpu.SemaphoreType.DMA((1,)), pltpu.SemaphoreType.DMA((2,))],
        compiler_params=SMALL,
        cost_estimate=cost(LONG),
        name="outgoing",
    )(place, labels, held)


def halves_kernel(own_ref, next_ref, rows_ref, outer_ref, inner_ref, labels, sem):
    count, width = rows_ref.shape
    copies = fetch(
        sem,
        (own_ref, labels.at[pl.ds(0, 1)]),
        (next_ref, labels.at[pl.ds(1, 1)]),
        (rows_ref.at[:, pl.ds(0, BLK)], outer_ref.at[pl.ds(0, count), pl.ds(0, BLK)]),
        (rows_ref.at[:, pl.ds(width - BLK, BLK)], outer_ref.at[pl.ds(0, count), pl.ds(BLK, BLK)]),
        (rows_ref.at[:, pl.ds(BLK, width - 2 * BLK)], inner_ref),
    )
    wait(copies[:2])
    index = lax.broadcasted_iota(jnp.int32, (EXTRA, count), 0)
    rows = jnp.where(index == 0, labels[0:1], jnp.where(index == 1, labels[1:2], 0))
    outer_ref[count : count + EXTRA, :count] = rows.astype(F32).astype(BF16)
    outer_ref[count : count + EXTRA, count:] = jnp.zeros((EXTRA, 2 * BLK - count), BF16)
    wait(copies[2:])


def halves(own_labels, next_labels, rows):
    count, width = rows.shape
    return pl.pallas_call(
        halves_kernel,
        out_shape=(
            jax.ShapeDtypeStruct((count + EXTRA, 2 * BLK), rows.dtype),
            jax.ShapeDtypeStruct((count, width - 2 * BLK), rows.dtype),
        ),
        in_specs=[HBM] * 3,
        out_specs=(VMEM, VMEM),
        scratch_shapes=[pltpu.VMEM((2, count), jnp.int32), pltpu.SemaphoreType.DMA((5,))],
        compiler_params=SMALL,
        cost_estimate=cost(1),
        name="halves",
    )(own_labels, next_labels, rows)


def early_kernel(own_label, next_label, own_ref, other_ref, sums_ref, labels, own, other, sem):
    width = own_ref.shape[1]
    copies = fetch(
        sem,
        (own_label, labels.at[pl.ds(0, 1)]),
        (next_label, labels.at[pl.ds(1, 1)]),
        (own_ref, own),
        (other_ref, other),
    )
    wait(copies)
    pairs = [labels.at[p : p + 1] for p in range(2)]
    sums, _ = class_sums(pairs, [own, other], slice(0, width))
    sums_ref[...] = sums


def early_sums(own_labels, next_labels, own, other):
    count, width = own.shape
    return pl.pallas_call(
        early_kernel,
        out_shape=jax.ShapeDtypeStruct((C, width), F32),
        in_specs=[HBM] * 4,
        out_specs=VMEM,
        scratch_shapes=[
            pltpu.VMEM((2, count), jnp.int32),
            pltpu.VMEM((count, width), BF16),
            pltpu.VMEM((count, width), BF16),
            pltpu.SemaphoreType.DMA((4,)),
        ],
        compiler_params=SMALL,
        cost_estimate=cost(LONG),
        name="early_sums",
    )(own_labels, next_labels, own, other)


def four_labels(labels, outer):
    count = labels.shape[1]
    late = outer[count : count + EXTRA, :count].astype(F32)
    return labels[0:1].astype(F32), labels[1:2].astype(F32), late[0:1], late[1:2]


def edges_kernel(place_ref, own_ref, next_ref, early_ref, third_ref, outer_ref, near_ref, far_ref,
                 labels, third, outer, sem):
    count, width = third_ref.shape
    copies = fetch(
        sem,
        (own_ref, labels.at[pl.ds(0, 1)]),
        (next_ref, labels.at[pl.ds(1, 1)]),
        (outer_ref, outer),
        (third_ref.at[:, pl.ds(0, BLK)], third.at[:, pl.ds(0, BLK)]),
        (third_ref.at[:, pl.ds(width - BLK, BLK)], third.at[:, pl.ds(BLK, BLK)]),
    )
    wait(copies[:3])
    hots = [onehot_rows(label) for label in four_labels(labels, outer)]
    counts = sum(jnp.sum(hot, axis=1, keepdims=True) for hot in hots)
    late = jnp.dot(hots[3].astype(BF16), outer[:count, :], preferred_element_type=F32)
    wait(copies[3:])
    late = late + jnp.dot(hots[2].astype(BF16), third[...], preferred_element_type=F32)
    first = (early_ref[:, :BLK] + late[:, :BLK]) / counts
    last = (early_ref[:, width - BLK :] + late[:, BLK:]) / counts

    @pl.when(place_ref[0] // 4 % 2 == 0)
    def _():
        near_ref[...] = last
        far_ref[...] = first

    @pl.when(place_ref[0] // 4 % 2 != 0)
    def _():
        near_ref[...] = first
        far_ref[...] = last


def edge_means(place, own_labels, next_labels, early, third, outer):
    edge = jax.ShapeDtypeStruct((C, BLK), F32)
    count = third.shape[0]
    return pl.pallas_call(
        edges_kernel,
        out_shape=(edge, edge),
        in_specs=[SMEM, HBM, HBM, VMEM, HBM, HBM],
        out_specs=(VMEM, VMEM),
        scratch_shapes=[
            pltpu.VMEM((2, count), jnp.int32),
            pltpu.VMEM((count, 2 * BLK), BF16),
            pltpu.VMEM(outer.shape, BF16),
            pltpu.SemaphoreType.DMA((5,)),
        ],
        compiler_params=SMALL,
        cost_estimate=cost(LONG),
        name="edge_means",
    )(place, own_labels, next_labels, early, third, outer)


def means_kernel(own_ref, next_ref, early_ref, third_ref, outer_ref, inner_ref,
                 means_ref, fourth_ref, labels_ref, labels, third, outer, inner, sem):
    count, width = third_ref.shape
    wait(
        fetch(
            sem,
            (own_ref, labels.at[pl.ds(0, 1)]),
            (next_ref, labels.at[pl.ds(1, 1)]),
            (third_ref, third),
            (outer_ref, outer),
            (inner_ref, inner),
        )
    )
    groups = four_labels(labels, outer)
    hots = [onehot_rows(label) for label in groups]
    counts = sum(jnp.sum(hot, axis=1, keepdims=True) for hot in hots)
    fourth = jnp.concatenate([outer[:count, :BLK], inner[...], outer[:count, BLK:]], axis=1)
    fourth_ref[...] = fourth
    sums = early_ref[...] + jnp.dot(hots[2].astype(BF16), third[...], preferred_element_type=F32)
    sums = sums + jnp.dot(hots[3].astype(BF16), fourth, preferred_element_type=F32)
    means_ref[...] = sums / counts
    for p, label in enumerate(groups):
        labels_ref[p : p + 1, :] = label


def class_means(own_labels, next_labels, early, third, outer, inner):
    whole = jax.ShapeDtypeStruct(early.shape, F32)
    count = third.shape[0]
    return pl.pallas_call(
        means_kernel,
        out_shape=(
            whole,
            jax.ShapeDtypeStruct(third.shape, third.dtype),
            jax.ShapeDtypeStruct((4, count), F32),
        ),
        in_specs=[HBM, HBM, VMEM, HBM, HBM, HBM],
        out_specs=(VMEM,) * 3,
        scratch_shapes=[
            pltpu.VMEM((2, count), jnp.int32),
            pltpu.VMEM(third.shape, BF16),
            pltpu.VMEM(outer.shape, BF16),
            pltpu.VMEM(inner.shape, BF16),
            pltpu.SemaphoreType.DMA((5,)),
        ],
        compiler_params=MIDDLE,
        cost_estimate=cost(10**9),
        name="class_means",
    )(own_labels, next_labels, early, third, outer, inner)


def stack_kernel(groups, role_ref, *refs):
    *sources, out_ref, sem = refs
    groups = (sources[: groups[0]], sources[groups[0] :])

    def pairs(group):
        start = 0
        for ref in group:
            yield ref, out_ref.at[pl.ds(start, ref.shape[0])]
            start += ref.shape[0]

    for owner, group in zip((True, False), groups, strict=True):

        @pl.when((role_ref[0] % 4 == 0) == owner)
        def _():
            wait(fetch(sem, *pairs(group)))


def stack(role, own, other):
    rows = sum(array.shape[0] for array in own)
    groups = (len(own), len(other))
    return pl.pallas_call(
        lambda *refs: stack_kernel(groups, *refs),
        out_shape=jax.ShapeDtypeStruct((rows, own[0].shape[1]), own[0].dtype),
        in_specs=[SMEM] + [ANY] * sum(groups),
        out_specs=ANY,
        scratch_shapes=[pltpu.SemaphoreType.DMA((max(groups),))],
        compiler_params=SMALL,
        cost_estimate=cost(1),
        name="stack",
    )(role, *own, *other)


def bands_kernel(precision, bands, sem):
    wait(fetch(sem, *[(precision.at[k], bands.at[:, pl.ds(k * BLK, BLK)]) for k in range(3)]))


def bands_beside(precision):
    width = precision.shape[1]
    return pl.pallas_call(
        bands_kernel,
        out_shape=jax.ShapeDtypeStruct((width, 3 * BLK), BF16),
        in_specs=[HBM],
        out_specs=VMEM,
        scratch_shapes=[pltpu.SemaphoreType.DMA((3,))],
        compiler_params=SMALL,
        cost_estimate=cost(1),
        name="bands_beside",
    )(precision)


def white_kernel(place_ref, held_ref, near_ref, far_ref, means_ref, near_means, far_means,
                 held_labels, bands, white_ref, score_ref, held, means):
    width = held_ref.shape[1]
    held[:, BLK : BLK + width] = held_ref[...]
    means[:, BLK : BLK + width] = means_ref[...]
    sides = (slice(0, BLK), slice(BLK + width, 2 * BLK + width))
    for odd, (far_side, near_side) in enumerate((sides, sides[::-1])):

        @pl.when(place_ref[0] // 4 % 2 == odd)
        def _():
            held[:, near_side] = near_ref[...]
            means[:, near_side] = near_means[...]

        @pl.when(place_ref[0] // 4 == odd)
        def _():
            held[:, far_side] = far_ref[...]
            means[:, far_side] = far_means[...]

        @pl.when(place_ref[0] // 4 == odd + 2)
        def _():
            held[:, far_side] = jnp.zeros(far_ref.shape, BF16)
            means[:, far_side] = jnp.zeros(far_means.shape, F32)

    onehot = onehot_rows(held_labels[...]).astype(BF16)
    picked = sum(contract_rows(onehot, piece) for piece in split3(means[...]))
    centred = held[...].astype(F32) - picked
    pieces = split3(centred)[:2]
    score = jnp.zeros((held_ref.shape[0], 128), F32)
    for m in range(width // BLK):
        inside = slice(m * BLK, (m + 1) * BLK)
        window = slice(m * BLK, (m + 3) * BLK)
        band = bands[inside, :]
        image = sum(contract_columns(piece[:, window], band) for piece in reversed(pieces))
        white_ref[:, inside] = image.astype(BF16)
        product = centred[:, (m + 1) * BLK : (m + 2) * BLK] * image
        for lanes in range(0, BLK, 128):
            score = score + product[:, lanes : lanes + 128]
    score_ref[...] = jnp.sum(score.T, axis=0, keepdims=True)


def whiten(place, held, near, far, means, near_means, far_means, held_labels, precision):
    count, width = held.shape
    return pl.pallas_call(
        white_kernel,
        out_shape=(
            jax.ShapeDtypeStruct((count, width), BF16),
            jax.ShapeDtypeStruct((1, count), F32),
        ),
        in_specs=[SMEM] + [VMEM] * 8,
        out_specs=(VMEM, VMEM),
        scratch_shapes=[
            pltpu.VMEM((count, width + 2 * BLK), BF16),
            pltpu.VMEM((C, width + 2 * BLK), F32),
        ],
        compiler_params=MEDIUM,
        cost_estimate=cost(LONG),
        name="whiten",
    )(place, held, near, far, means, near_means, far_means, held_labels, precision)


def choose(role_ref, sem, near, far, target):
    here = role_ref[0] % 2 == 0

    @pl.when(here)
    def _():
        fetch(sem, (near, target))

    @pl.when(jnp.logical_not(here))
    def _():
        fetch(sem, (far, target))

    return pltpu.make_async_copy(near, target, sem.at[0])


def centre_kernel(labels_ref, means_ref, *refs):
    *rows, most_ref, last_ref = refs
    count = rows[0].shape[0]
    most = most_ref.shape[0] // 2
    pieces = split3(means_ref[...])
    for p, ref in enumerate(rows):
        onehot = onehot_rows(labels_ref[p : p + 1]).astype(BF16)
        centred = ref[...].astype(F32) - sum(contract_rows(onehot, piece) for piece in pieces)
        high = centred.astype(BF16)
        low = (centred - high.astype(F32)).astype(BF16)
        into, first, second = (most_ref, p * count, most + p * count)
        if p == len(rows) - 1:
            into, first, second = (last_ref, 0, count)
        into[first : first + count, :] = high
        into[second : second + count, :] = low


def centre(labels, means, rows):
    count, width = rows[0].shape
    return pl.pallas_call(
        centre_kernel,
        out_shape=(
            jax.ShapeDtypeStruct((2 * (len(rows) - 1) * count, width), BF16),
            jax.ShapeDtypeStruct((2 * count, width), BF16),
        ),
        in_specs=[VMEM] * (2 + len(rows)),
        out_specs=(VMEM, VMEM),
        compiler_params=MIDDLE,
        cost_estimate=cost(1),
        name="centre",
    )(labels, means, *rows)


def most_kernel(role_ref, left, near, far, total_ref, right, sem):
    most, width = near.shape
    choose(role_ref, sem, near, far, right).wait()
    for t in range(0, width, BLK):
        high = contract_rows(left[:most, t : t + BLK], right[...])
        total_ref[t : t + BLK, :] = high + contract_rows(left[most:, t : t + BLK], right[...])


def gram_most(role, centred, near, far):
    width = near.shape[1]
    return pl.pallas_call(
        most_kernel,
        out_shape=jax.ShapeDtypeStruct((width, width), F32),
        in_specs=[SMEM, VMEM, ANY, ANY],
        out_specs=VMEM,
        scratch_shapes=[pltpu.VMEM(near.shape, BF16), pltpu.SemaphoreType.DMA((1,))],
        compiler_params=MIDDLE,
        cost_estimate=cost(LONG),
        name="gram_most",
    )(role, centred, near, far)


def last_kernel(scale, features, role_ref, total_ref, last_ref, near, far, own, *refs):
    *others, out_ref, distance_ref, right, tiles, sem, out_sem = refs
    count, width = near.shape
    arrival = choose(role_ref, sem, near, far, right)
    beside, across, beyond = [ref[...] for ref in others]
    distance_ref[...] = ((own[...] + beside) + (across + beyond)) / features
    arrival.wait()
    stores = []
    for k, t in enumerate(range(0, width, TILE)):
        part = contract_rows(last_ref[:count, t : t + TILE], right[...])
        part = part + contract_rows(last_ref[count:, t : t + TILE], right[...])
        tiles[t : t + TILE, :] = (total_ref[t : t + TILE, :] + part) * scale
        stores.append(
            pltpu.make_async_copy(
                tiles.at[pl.ds(t, TILE)], out_ref.at[pl.ds(t, TILE)], out_sem.at[k]
            )
        )
        stores[-1].start()
    wait(stores)


def gram_last(role, total, last, near, far, scores, scale, features):
    count, width = near.shape
    return pl.pallas_call(
        lambda *refs: last_kernel(scale, features, *refs),
        out_shape=(
            jax.ShapeDtypeStruct((width, width), F32),
            jax.ShapeDtypeStruct(scores[0].shape, F32),
        ),
        in_specs=[SMEM, VMEM, VMEM, ANY, ANY] + [VMEM] * len(scores),
        out_specs=(HBM, VMEM),
        scratch_shapes=[
            pltpu.VMEM((count, width), BF16),
            pltpu.VMEM((width, width), F32),
            pltpu.SemaphoreType.DMA((1,)),
            pltpu.SemaphoreType.DMA((width // TILE,)),
        ],
        compiler_params=MIDDLE,
        cost_estimate=cost(LONG),
        name="gram_last",
    )(role, total, last, near, far, *scores)


def four_by_four(train_rows, train_labels, held_rows, held_labels, precision):
    count, width = train_rows.shape
    n = 4
    tie = lax.optimization_barrier
    flip = {k: [(i, i ^ k) for i in range(n)] for k in (1, 2, 3)}
    inward = [(1, 2), (2, 1)]
    feat = lax.axis_index("feat")
    at_end = (feat == 0) | (feat == n - 1)
    role = (lax.axis_index("dp") ^ feat) + n * (feat % 2) + 2 * n * at_end.astype(jnp.int32)
    role = role.astype(jnp.int32).reshape(1)

    def hop(array, *moves):
        pairs = [(d * n + (d ^ s), d * n + (d ^ e)) for d in range(n) for s, e in moves]
        return lax.ppermute(array, ("dp", "feat"), pairs)

    across_own = hop(train_rows, (0, 2))
    third = lax.ppermute(train_rows, "dp", flip[1])
    second = lax.ppermute(train_rows, "dp", flip[2])
    own_labels, near, far = outgoing(role, train_labels.reshape(1, count), held_rows)
    near = lax.ppermute(near, "feat", flip[1])
    far = lax.ppermute(far, "feat", flip[3])
    near, own_labels = tie((near, own_labels))
    next_labels = lax.ppermute(own_labels, "dp", flip[2])
    second, third, across_own, near, far, next_labels = tie(
        (second, third, across_own, near, far, next_labels)
    )
    second_outer, second_inner = halves(own_labels, next_labels, second)
    outer = lax.ppermute(second_outer, "dp", flip[1])
    inner = lax.ppermute(second_inner, "dp", flip[1])
    early = early_sums(own_labels, next_labels, train_rows, second)
    early, *sent = tie((early, second, third))
    own_most = stack(role, sent, sent)
    across_most = hop(own_most, (0, 2))
    near_edge, far_edge = edge_means(role, own_labels, next_labels, early, third, outer)
    near_means = lax.ppermute(near_edge, "feat", flip[1])
    far_means = lax.ppermute(far_edge, "feat", inward)
    inner, near_edge, bands = tie((inner, near_edge, bands_beside(precision)))
    means, fourth, labels = class_means(own_labels, next_labels, early, third, outer, inner)
    across_last = hop(fourth, (0, 2))
    rows = [train_rows, second, third, fourth]
    near_most = stack(role, rows[:3], [across_own, across_most])
    far_most = lax.ppermute(near_most, "feat", flip[1])
    most, last = centre(labels, means, rows)
    most, last, means = tie((most, last, means))
    white, score = whiten(
        role, held_rows, near, far, means, near_means, far_means, held_labels.reshape(1, -1), bands
    )
    score, most = tie((score, most))
    total = gram_most(role, most, near_most, far_most)
    beside = lax.ppermute(score, "feat", flip[1])
    beside, across_last = tie((beside, across_last))
    near_last = stack(role, [fourth], [across_last])
    far_last = lax.ppermute(near_last, "feat", flip[1])
    scores = [score, beside] + [lax.ppermute(score, "feat", flip[k]) for k in (2, 3)]
    cov, distance = gram_last(
        role, total, last, near_last, far_last, scores, 1.0 / (n * count - C), float(n * width)
    )
    return cov, white, distance.reshape(-1)


def solution(mesh):
    fits = mesh.shape["dp"] == 4 and mesh.shape["feat"] == 4
    return jax.shard_map(
        four_by_four if fits else body,
        mesh=mesh,
        in_specs=(
            P(("layer", "dp"), "feat"),
            P(("layer", "dp"), None),
            P(("layer", "dp"), "feat"),
            P(("layer", "dp")),
            P("layer", "feat", None),
        ),
        out_specs=(P(("layer", "feat"), "dp"), P(("layer", "dp"), "feat"), P(("layer", "dp"))),
        check_vma=False,
    )
```
